128 devices in a mesh: seq: 8 (over y, core), exp: 16 (over z, x).
Axes of the slice: x: 4, y: 4, z: 4, core: 2. Of those that a mesh axis runs over, the one named last changes fastest.
Arguments:
- signal: float32 [16384, 8192], P('seq', 'exp'), may hold values from -6 to 6
- out_gate: bfloat16 [16384, 8192], P('seq', 'exp'), may hold values from -6 to 6
- state_in: float32 [16384, 16], P('seq'), may hold values from -1 to 1
- state_out: float32 [16384, 16], P('seq'), may hold values from -1 to 1
- step_size: float32 [128, 16384], P('exp', 'seq'), may hold values from 0.5 to 2
- head_log_decay: float32 [128, 16384], P('exp', 'seq'), may hold values from 0 to 1
- skip_gain: float32 [128], P('exp'), may hold values from 0.5 to 1.5
- norm_gain: float32 [8192], P('exp'), may hold values from 0.1 to 1.9
- residual: bfloat16 [16384, 8192], P('seq', 'exp'), may hold values from -6 to 6
- route: int32 [16384, 2], P(('seq', 'exp')), may hold values from 0 to 15, all different within a row; in each aligned block of 128 rows (0 to 127, 128 to 255, ...) at most 32 rows name the same one
- combine_weight: float32 [2, 16384], P(None, ('seq', 'exp')), may hold values from 0.2 to 1
- up_first: bfloat16 [16, 256, 768], P('exp'), may hold values from -0.375 to 0.375
- up_second: bfloat16 [16, 256, 256], P('exp'), may hold values from -0.375 to 0.375
- gate_first: bfloat16 [16, 256, 768], P('exp'), may hold values from -0.375 to 0.375
- gate_second: bfloat16 [16, 256, 256], P('exp'), may hold values from -0.375 to 0.375
- down_first: bfloat16 [16, 256, 256], P('exp'), may hold values from -0.375 to 0.375
- down_second: bfloat16 [16, 768, 256], P('exp'), may hold values from -0.21875 to 0.21875
Outputs:
- mixed: bfloat16 [16384, 8192], P('seq', 'exp')
- routed: bfloat16 [16384, 8192], P(('seq', 'exp'))
The draws below stay inside these ranges and needn't reach their ends.
Inputs may be any that keep to these rules, and one draw needn't show every extreme that they name: `route`: each row names 2 different experts; among the rows of one device no expert is named by more than 32 rows, a bound that some block reaches.
All inputs are finite; a program needn't handle non-finite values.
Results may differ from the reference program's by a relative error of at most 0.029.
Values may be sent and summed in bfloat16 or wider, within the bound.
A program may use at most 192 MiB of HBM per device.

```python
import math
import jax
import jax.numpy as jnp
import numpy as np
from jax import lax

D = 8192
NSTATE = 16
HEAD_DIM = 64
GROUP = 256
RANK = 8
FIRST_MODE = 32
HID_MODE = 32
TOP = 2
ROWS_DEV = 128
SEQ = 16384
HEADS = 128
EXPERTS = 16
CAP = 32
SECOND_MODE = 256
HID_REST = 768


def draw_head_log_decay(key, part):
    key = jax.random.fold_in(key, 17)
    keys = jax.random.split(key, 5)
    fast_cut = 8
    picks = jax.random.randint(keys[0], (HEADS, 1), 0, 16)
    fast_rate = jnp.exp(jax.random.uniform(keys[1], (HEADS, 1), jnp.float32, math.log(1.0 / 60.0), math.log(1.0 / 20.0)))
    slow_rate = 0.5 / SEQ
    baseline_value = jnp.where(picks < fast_cut, fast_rate, slow_rate)
    coarse_estimate = jnp.exp(jax.random.uniform(keys[2], (HEADS, SEQ), jnp.float32, -math.log(2.0), math.log(2.0)))
    slot_locations = jax.random.randint(keys[3], (HEADS, 1, 2), 0, SEQ)
    loss_values = jax.random.uniform(keys[4], (HEADS, 1, 2), jnp.float32, 0.22, 0.69)
    expert_positions = jnp.arange(SEQ, dtype=jnp.int32)[None, :, None]
    token_groups = jnp.sum(jnp.where(expert_positions == slot_locations, loss_values, 0.0), axis=2)
    return (baseline_value * coarse_estimate + token_groups).astype(jnp.float32)


def block_scale(own_key, shape, cuts, low, high):
    factor_of = 1.0
    for dim, blocks in cuts:
        steps = jax.random.uniform(jax.random.fold_in(jax.random.fold_in(own_key, 6), dim), (blocks,), jnp.float32, low / len(cuts), high / len(cuts))
        factor_of = factor_of * jnp.repeat(jnp.exp(steps), shape[dim] // blocks).reshape((-1,) + (1,) * (len(shape) - 1 - dim))
    return factor_of


def routed_block(stream_key, own, number, rows, number_of, top, reach, slope):
    sequence = jax.random.permutation(stream_key, number_of)
    crowded, common = portions_of(number_of, rows * top, reach, slope, True), portions_of(number_of, rows * top, reach, slope, False)
    places = jnp.arange(number_of)

    def named(tallies, turn):
        used = int((tallies > 0).sum())
        fixed = max(1, used // 4)
        passed = fixed + (places - fixed + turn * (used - fixed)) % max(1, number_of - fixed)
        return jnp.zeros((number_of,), jnp.int32).at[sequence[jnp.where(places < fixed, places, passed)]].set(jnp.asarray(tallies, jnp.int32))

    tallies = jnp.where(number % 4 == 0, named(crowded, number // 4), named(common, number - number // 4 - 1))
    mixed = jax.random.permutation(jax.random.fold_in(own, 3), number_of)
    donor, receiver = mixed[0:number_of // 2 * 2:2], mixed[1:number_of // 2 * 2:2]
    margin = jnp.minimum(tallies[donor] - 1, reach - tallies[receiver]) // 2
    margin = jnp.where((donor == sequence[0]) | (receiver == sequence[0]) | (tallies[receiver] == 0), 0, jnp.maximum(margin, 0))
    passed = jax.random.randint(jax.random.fold_in(own, 4), (number_of // 2,), 0, 1 << 20) % (margin + 1)
    tallies = tallies.at[donor].add(-passed).at[receiver].add(passed)
    labels = jnp.searchsorted(jnp.cumsum(tallies), jnp.arange(rows * top), side="right").astype(jnp.int32)
    grid = labels.reshape(top, rows).T
    grid = grid[jax.random.permutation(jax.random.fold_in(own, 1), rows)]
    turn = jax.random.randint(jax.random.fold_in(own, 2), (rows, 1), 0, top)
    return jnp.take_along_axis(grid, (jnp.arange(top)[None, :] + turn) % top, axis=1)


def portions_of(number_of, total, most, slope, full):
    loads = [(1 << 20) // math.isqrt(standing ** slope) + 1 for standing in range(1, number_of + 1)]
    largest = most if full else min(most, max(-(-total // number_of), total * loads[0] // sum(loads)))
    least = 1 if total - largest >= number_of - 1 else 0
    counts, spare = [largest] + [least] * (number_of - 1), total - largest - least * (number_of - 1)
    while spare > 0:
        movable = [i for i in range(1, number_of) if counts[i] < largest] or [i for i in range(1, number_of) if counts[i] < most]
        pool, budget = sum([loads[i] for i in movable]), spare
        for i in movable:
            more = min(most - counts[i], max(1, budget * loads[i] // pool), spare)
            counts[i] = counts[i] + more
            spare = spare - more
    return np.array(counts)


def normal_values(rng, shape, deviation, reach, cuts=(), held_as=jnp.bfloat16):
    gain = block_scale(rng, shape, cuts, -0.22, 0.18) if cuts else 1.0
    entries = jax.random.normal(rng, shape, jnp.float32) * deviation * gain
    return jnp.minimum(jnp.maximum(entries, -reach), reach).astype(held_as)


def setup_inputs(seed: int = 0) -> dict:
    key_of = jax.random.split(jax.random.key(seed), 18)
    signal = normal_values(key_of[0], (SEQ, HEADS * HEAD_DIM), 1.0, 6.0, ((0, 8), (1, 16)), jnp.float32)
    out_gate = normal_values(key_of[1], (SEQ, HEADS * HEAD_DIM), 1.0, 6.0, ((0, 8), (1, 16)))
    state_in = normal_values(key_of[2], (SEQ, NSTATE), 0.15, 1.0, ((0, 8),), jnp.float32)
    state_out = normal_values(key_of[3], (SEQ, NSTATE), 0.15, 1.0, ((0, 8),), jnp.float32)
    step_size = jnp.clip(jnp.exp(math.log(2.0) - 1.3862944 * jax.random.uniform(key_of[4], (HEADS, SEQ), jnp.float32) ** block_scale(key_of[4], (HEADS, SEQ), ((0, 16), (1, 8)), -0.2, 0.2)), 0.5, 2.0)
    head_log_decay = draw_head_log_decay(jax.random.fold_in(key_of[17], 71), 0)
    skip_gain = jnp.clip(0.5 + 1.0 * jax.random.uniform(key_of[6], (HEADS,), jnp.float32) ** block_scale(key_of[6], (HEADS,), ((0, 16),), -0.2, 0.2), 0.5, 1.5)
    norm_gain = jnp.clip(1.0 + 0.18 * jax.random.normal(key_of[7], (HEADS * HEAD_DIM,), jnp.float32), 0.1, 1.9)
    residual = normal_values(key_of[8], (SEQ, D), 1.0, 6.0, ((0, 8), (1, 16)))
    route_keys = jax.random.split(jax.random.fold_in(key_of[9], 1), SEQ // ROWS_DEV)
    route_turns = jax.random.permutation(jax.random.fold_in(key_of[9], 3), SEQ // ROWS_DEV)
    route = jax.vmap(lambda own, number: routed_block(jax.random.fold_in(key_of[9], 2), own, number, ROWS_DEV, EXPERTS, TOP, CAP, 2))(route_keys, route_turns).reshape((SEQ, TOP))
    combine_weight = jnp.clip(0.2 + 0.8 * jax.random.uniform(key_of[10], (TOP, SEQ), jnp.float32) ** block_scale(key_of[10], (TOP, SEQ), ((1, 128),), -0.2, 0.2), 0.2, 1.0)
    up_first = normal_values(key_of[11], (EXPERTS, FIRST_MODE * RANK, HID_REST), (FIRST_MODE * RANK) ** -0.5, 0.375, ((0, 16),))
    up_second = normal_values(key_of[12], (EXPERTS, SECOND_MODE, HID_MODE * RANK), SECOND_MODE ** -0.5, 0.375, ((0, 16),))
    gate_first = normal_values(key_of[13], (EXPERTS, FIRST_MODE * RANK, HID_REST), (FIRST_MODE * RANK) ** -0.5, 0.375, ((0, 16),))
    gate_second = normal_values(key_of[14], (EXPERTS, SECOND_MODE, HID_MODE * RANK), SECOND_MODE ** -0.5, 0.375, ((0, 16),))
    down_first = normal_values(key_of[15], (EXPERTS, HID_MODE * RANK, SECOND_MODE), (HID_MODE * RANK) ** -0.5, 0.375, ((0, 16),))
    down_second = normal_values(key_of[16], (EXPERTS, HID_REST, FIRST_MODE * RANK), HID_REST ** -0.5, 0.21875, ((0, 16),))
    return {"signal": signal, "out_gate": out_gate, "state_in": state_in, "state_out": state_out, "step_size": step_size, "head_log_decay": head_log_decay, "skip_gain": skip_gain, "norm_gain": norm_gain, "residual": residual, "route": route, "combine_weight": combine_weight, "up_first": up_first, "up_second": up_second, "gate_first": gate_first, "gate_second": gate_second, "down_first": down_first, "down_second": down_second}


HIGH = lax.Precision.HIGHEST
EPS = 1e-05

def block_pass(current, block):
    signal_part, input_part, output_part, step_part, rate_part = block
    length = rate_part.shape[1]
    running = jnp.cumsum(rate_part, axis=1)
    below_diag = jnp.arange(length)[:, None] >= jnp.arange(length)[None, :]
    spread = jnp.where(below_diag[None], running[:, :, None] - running[:, None, :], 0.0)
    decay = jnp.where(below_diag[None], jnp.exp(-spread), 0.0)
    scores = jnp.dot(output_part, input_part.T, precision=HIGH)
    mixing = decay * scores[None] * step_part[:, None, :]
    local_part = jnp.einsum('hts,shp->thp', mixing, signal_part, precision=HIGH)
    entering = jnp.exp(-running)
    carried = jnp.einsum('tn,hpn->thp', output_part, current, precision=HIGH) * entering.T[:, :, None]
    leaving = jnp.exp(running - running[:, -1:]) * step_part
    added_state = jnp.einsum('hs,shp,sn->hpn', leaving, signal_part, input_part, precision=HIGH)
    updated = entering[:, -1][:, None, None] * current + added_state
    return (updated, local_part + carried)

def sweep(signal_view, state_in, state_out, step_size, head_log_decay, current):
    length, heads, channels = signal_view.shape
    blocks = length // GROUP
    packed = (signal_view.reshape(blocks, GROUP, heads, channels), state_in.reshape(blocks, GROUP, -1), state_out.reshape(blocks, GROUP, -1), step_size.reshape(heads, blocks, GROUP).transpose(1, 0, 2), head_log_decay.reshape(heads, blocks, GROUP).transpose(1, 0, 2))
    current, outputs = lax.scan(block_pass, current, packed)
    return (current, outputs.reshape(length, heads, channels))

def normalize(rows):
    wide = rows.astype(jnp.float32)
    return (wide * lax.rsqrt(lax.optimization_barrier(jnp.mean(wide * wide, axis=1, keepdims=True)) + EPS)).astype(jnp.bfloat16)

def tensor_train(rows, first, second, lead):
    number = rows.shape[0]
    rest = second.shape[0]
    rank_size = first.shape[0] // lead
    middle = second.shape[1] // rank_size
    partial_value = jnp.dot(rows.reshape(number * lead, rest), second, preferred_element_type=jnp.float32)
    partial_value = partial_value.reshape(number, lead, middle, rank_size).transpose(0, 2, 1, 3)
    partial_value = partial_value.reshape(number, middle, lead * rank_size).astype(jnp.bfloat16)
    result = jnp.einsum('mdk,kc->mdc', partial_value.astype(jnp.float32), first.astype(jnp.float32))
    return result.reshape(number, middle * first.shape[1])

def expert(rows, cores):
    up_a, up_b, gate_a, gate_b, down_a, down_b = cores
    upward = tensor_train(rows, up_a, up_b, FIRST_MODE)
    gating = tensor_train(rows, gate_a, gate_b, FIRST_MODE)
    hidden = (jax.nn.silu(gating) * upward).astype(jnp.bfloat16)
    return tensor_train(hidden, down_a, down_b, HID_MODE).astype(jnp.bfloat16)

def reference(signal, out_gate, state_in, state_out, step_size, head_log_decay, skip_gain, norm_gain, residual, route, combine_weight, up_first, up_second, gate_first, gate_second, down_first, down_second):
    heads = skip_gain.shape[0]
    length = signal.shape[0]
    signal_view = signal.reshape(length, heads, HEAD_DIM)
    start_state = jnp.zeros((heads, HEAD_DIM, NSTATE), jnp.float32)
    final_state, outputs = sweep(signal_view, state_in, state_out, step_size, head_log_decay, start_state)
    outputs = outputs + skip_gain[None, :, None] * signal_view
    gated = outputs.reshape(length, heads * HEAD_DIM) * jax.nn.silu(out_gate.astype(jnp.float32))
    mean_sq = lax.optimization_barrier(jnp.mean(gated * gated, axis=1))
    mixed = (gated * lax.rsqrt(mean_sq + EPS)[:, None] * norm_gain[None, :]).astype(jnp.bfloat16)
    stream = (residual.astype(jnp.float32) + mixed.astype(jnp.float32)).astype(jnp.bfloat16)
    normed = normalize(stream)
    chosen = route.reshape(-1).astype(jnp.int32)
    shares = combine_weight.T.reshape(-1)
    span = 256
    start_acc = jnp.zeros(residual.shape, jnp.float32)

    def per_expert(accum, packed):
        number = packed[0]
        cores = packed[1:]
        match = chosen == number
        order = jnp.argsort(jnp.where(match, 0, 1).astype(jnp.int32), stable=True).astype(jnp.int32)
        total = jnp.sum(match.astype(jnp.int32))

        def one_block(index, accum):
            first_row = (jnp.asarray(index) * span).astype(jnp.int32)
            picks = lax.dynamic_slice_in_dim(order, first_row, span)
            valid = first_row + jnp.arange(span, dtype=jnp.int32) < total
            owners_row = (picks // TOP).astype(jnp.int32)
            result = expert(normed[owners_row], cores).astype(jnp.float32)
            scale = jnp.where(valid, shares[picks], 0.0)
            return accum.at[owners_row].add(result * scale[:, None])
        accum = lax.fori_loop(0, (total + span - 1) // span, one_block, accum)
        return (accum, None)
    packed = (jnp.arange(EXPERTS, dtype=jnp.int32), up_first, up_second, gate_first, gate_second, down_first, down_second)
    accum, _ = lax.scan(per_expert, start_acc, packed)
    return (mixed, accum.astype(jnp.bfloat16))
```

```python
import jax
import jax.numpy as jnp
from jax import lax
from jax.experimental import pallas as pl
from jax.experimental.pallas import tpu as pltpu
from jax.sharding import PartitionSpec as P

MESH = pl.DeviceIdType.MESH
HIGH = lax.Precision.HIGHEST
EPS = 1e-05
F32, BF16 = jnp.float32, jnp.bfloat16
CH = 128
NCH = 16
WID = 512
SLOT = 32
HALF = 8
PACK = 3072


def iota(shape, dim):
    return lax.broadcasted_iota(jnp.int32, shape, dim)


def dot(a, b, ca, cb, precision=None):
    return lax.dot_general(
        a, b, (((ca,), (cb,)), ((), ())), precision=precision, preferred_element_type=F32
    )


def halves(v):
    hi = v.astype(BF16)
    return hi, (v - hi.astype(F32)).astype(BF16)


def rcopy(src, dst, send, recv, dev):
    return pltpu.make_async_remote_copy(
        src_ref=src, dst_ref=dst, send_sem=send, recv_sem=recv, device_id=dev, device_id_type=MESH
    )


def silu(v):
    return v * (0.5 + 0.5 * jnp.tanh(0.5 * v))


def mixer_kernel(
    sig, gate, b_in, c_out, dt, rate, skip, ngain, resid, info,
    mixed, tok, infos,
    bx, sraw, gated, amat, bmat, gtot, gend, gmid, st_loc, st_buf, ssq, land, sendb, inv_s, info_l,
    st_s, st_r, sq_s, sq_r, tk_s, tk_r, nb_s, nb_r, in_s, in_r,
):
    me_e, me_s = lax.axis_index("exp"), lax.axis_index("seq")
    core = lax.rem(me_s, 2)
    sib = me_s + 1 - 2 * core

    barrier = pltpu.get_barrier_semaphore()
    for d in range(1, 16):
        pl.semaphore_signal(barrier, inc=1, device_id={"exp": lax.rem(me_e + d, 16)}, device_id_type=MESH)
    for d in range(1, 8):
        pl.semaphore_signal(barrier, inc=1, device_id={"seq": lax.rem(me_s + d, 8)}, device_id_type=MESH)
    pl.semaphore_wait(barrier, 22)
    info_cp = rcopy(info, info_l, in_s, in_r, {"seq": sib})
    info_cp.start()

    rate2 = jnp.concatenate([rate[:, c * CH : (c + 1) * CH] for c in range(NCH)], axis=0)
    dt2 = jnp.concatenate([dt[:, c * CH : (c + 1) * CH] for c in range(NCH)], axis=0)
    tri = (iota((CH, CH), 0) >= iota((CH, CH), 1)).astype(F32)
    run = dot(tri, rate2, 1, 1, HIGH)
    mid, end = run[63:64, :], run[127:128, :]
    av = jnp.exp(mid - run)
    bv = jnp.exp(run - mid) * dt2.T
    ah, al = halves(av)
    bh, bl = halves(bv)
    amat[:, :CH], amat[:, CH:] = ah, al
    bmat[:, :CH], bmat[:, CH:] = bh, bl
    spread = ((iota((CH, WID), 0) & 7) == (iota((CH, WID), 1) >> 6)).astype(F32)
    own = (iota((NCH, CH), 1) >> 3) == iota((NCH, CH), 0)

    def rows_of(v):
        return dot(jnp.where(own, v, 0.0), spread, 1, 0, HIGH)

    gtot[...] = rows_of(jnp.exp(-end))
    gend[...] = rows_of(jnp.exp(mid - end))
    gmid[...] = rows_of(jnp.exp(-mid))
    all_end = dot(jnp.broadcast_to(end, (8, CH)), spread, 1, 0, HIGH)

    def picker(c):
        return ((iota((2 * CH, WID), 0) & (CH - 1)) == c * 8 + (iota((2 * CH, WID), 1) >> 6)).astype(BF16)

    def first(c, state):
        rows = pl.ds(pl.multiple_of(c * CH, CH), CH)
        x = (dot(bmat[...], picker(c), 1, 0) * sig[rows, :]).astype(BF16)
        bx[rows, :] = x
        s = dot(b_in[rows, :].astype(BF16), x, 0, 0)
        sraw[c] = s
        return gtot[pl.ds(c, 1), :] * state + gend[pl.ds(c, 1), :] * s

    state = lax.fori_loop(0, NCH, first, jnp.zeros((16, WID), F32))
    st_loc[0:16, :] = state
    st_loc[16:24, :] = jnp.exp(-all_end)
    st_buf[me_s] = st_loc[...]
    st_cp = []
    for d in range(1, 8):
        to = lax.rem(me_s + d, 8)
        st_cp.append(rcopy(st_loc, st_buf.at[me_s], st_s.at[d], st_r.at[me_s], {"seq": to}))
        st_cp[-1].start()
    for d in range(1, 8):
        frm = lax.rem(me_s + 8 - d, 8)
        rcopy(st_loc, st_buf.at[frm], st_s.at[d], st_r.at[frm], {"seq": frm}).wait_recv()

    state = jnp.zeros((16, WID), F32)
    for k in range(7):
        new = st_buf[k, 16:17, :] * state + st_buf[k, 0:16, :]
        state = jnp.where(k < me_s, new, state)

    low = iota((CH, CH), 0) >= iota((CH, CH), 1)
    skip_e = dot(jnp.broadcast_to(skip[...], (8, CH)), spread, 1, 0, HIGH)[0:1, :]
    ones = jnp.ones((8, WID), BF16)

    def second(c, state):
        rows = pl.ds(pl.multiple_of(c * CH, CH), CH)
        cm = c_out[rows, :].astype(BF16)
        scores = jnp.where(low, dot(cm, b_in[rows, :].astype(BF16), 1, 1), 0.0).astype(BF16)
        enter = (gmid[pl.ds(c, 1), :] * state).astype(BF16)
        y = dot(scores, bx[rows, :], 1, 0) + dot(cm, enter, 1, 0)
        y = y * dot(amat[...], picker(c), 1, 0) + skip_e * sig[rows, :]
        g = y * silu(gate[rows, :].astype(F32))
        gated[rows, :] = g
        ssq[me_e, pl.ds(c, 1), :] = dot(ones, (g * g).astype(BF16), 1, 1)[0:1, :]
        return gtot[pl.ds(c, 1), :] * state + gend[pl.ds(c, 1), :] * sraw[c]

    lax.fori_loop(0, NCH, second, state)

    sq_cp = []
    for d in range(1, 16):
        to = lax.rem(me_e + d, 16)
        sq_cp.append(rcopy(ssq.at[me_e], ssq.at[me_e], sq_s.at[d], sq_r.at[me_e], {"exp": to}))
        sq_cp[-1].start()
    for d in range(1, 16):
        frm = lax.rem(me_e + 16 - d, 16)
        rcopy(ssq.at[frm], ssq.at[frm], sq_s.at[d], sq_r.at[frm], {"exp": frm}).wait_recv()
    total = ssq[0]
    for k in range(1, 16):
        total = total + ssq[k]
    inv = lax.rsqrt(total * (1.0 / 8192.0) + EPS)
    inv_t = jnp.concatenate([inv, jnp.zeros((CH - NCH, CH), F32)], axis=0).T
    ih, il = halves(inv_t)
    inv_s[:, :CH], inv_s[:, CH:] = ih, il

    def third(c):
        rows = pl.ds(pl.multiple_of(c * CH, CH), CH)
        sel = ((iota((2 * CH, WID), 0) & (CH - 1)) == c).astype(BF16)
        m = (gated[rows, :] * dot(inv_s[...], sel, 1, 0) * ngain[...]).astype(BF16)
        mixed[rows, :] = m
        return (resid[rows, :].astype(F32) + m.astype(F32)).astype(BF16)

    def send_block(k, _):
        c = lax.rem(me_e + 1 + k, 16)
        sendb[c] = third(c)
        rcopy(sendb.at[c], land.at[me_e], tk_s.at[c], tk_r.at[me_e], {"exp": c}).start()
        return 0

    lax.fori_loop(0, 15, send_block, 0)
    land[me_e] = third(me_e)

    def squares(src):
        v = land[src].astype(F32)
        v = v * v
        return v[:, 0:128] + v[:, 128:256] + v[:, 256:384] + v[:, 384:512]

    def arrive(k, acc):
        src = lax.rem(me_e + 15 - k, 16)
        rcopy(sendb.at[src], land.at[src], tk_s.at[src], tk_r.at[src], {"exp": src}).wait_recv()
        return acc + squares(src)

    acc = lax.fori_loop(0, 15, arrive, squares(me_e))
    rs = lax.rsqrt(jnp.sum(acc, axis=1, keepdims=True) * (1.0 / 8192.0) + EPS)

    def normal(src, _):
        tok[0, src] = (land[src].astype(F32) * rs).astype(BF16)
        rcopy(tok.at[0, src], tok.at[1, src], nb_s.at[src], nb_r.at[src], {"seq": sib}).start()
        return 0

    lax.fori_loop(0, 16, normal, 0)
    info_cp.wait()
    shift = jnp.where(iota((8, CH), 0) < 2, (core * HALF).astype(F32), 0.0)
    infos[0] = info[...] - shift
    infos[1] = info_l[...] - shift

    def settle(src, _):
        rcopy(tok.at[0, src], tok.at[1, src], nb_s.at[src], nb_r.at[src], {"seq": sib}).wait()
        return 0

    lax.fori_loop(0, 16, settle, 0)
    for cp in st_cp:
        cp.wait_send()
    for cp in sq_cp:
        cp.wait_send()

    def sent(k, _):
        c = lax.rem(me_e + 1 + k, 16)
        rcopy(sendb.at[c], land.at[me_e], tk_s.at[c], tk_r.at[me_e], {"exp": c}).wait_send()
        return 0

    lax.fori_loop(0, 15, sent, 0)


def run_mixer(sig, gate, b_in, c_out, dt, rate, skip, ngain, resid, info):
    vm = pl.BlockSpec(memory_space=pltpu.VMEM)
    dma = pltpu.SemaphoreType.DMA
    return pl.pallas_call(
        mixer_kernel,
        out_shape=(
            jax.ShapeDtypeStruct((2048, WID), BF16),
            jax.ShapeDtypeStruct((2, 16, CH, WID), BF16),
            jax.ShapeDtypeStruct((2, 8, CH), F32),
        ),
        in_specs=[vm] * 10,
        out_specs=(vm, vm, vm),
        scratch_shapes=[
            pltpu.VMEM((2048, WID), BF16),
            pltpu.VMEM((NCH, 16, WID), F32),
            pltpu.VMEM((2048, WID), F32),
            pltpu.VMEM((CH, 2 * CH), BF16),
            pltpu.VMEM((CH, 2 * CH), BF16),
            pltpu.VMEM((NCH, WID), F32),
            pltpu.VMEM((NCH, WID), F32),
            pltpu.VMEM((NCH, WID), F32),
            pltpu.VMEM((24, WID), F32),
            pltpu.VMEM((8, 24, WID), F32),
            pltpu.VMEM((16, NCH, CH), F32),
            pltpu.VMEM((16, CH, WID), BF16),
            pltpu.VMEM((16, CH, WID), BF16),
            pltpu.VMEM((CH, 2 * CH), BF16),
            pltpu.VMEM((8, CH), F32),
            dma((8,)), dma((8,)), dma((16,)), dma((16,)), dma((16,)), dma((16,)), dma((16,)), dma((16,)),
            dma, dma,
        ],
        compiler_params=pltpu.CompilerParams(
            collective_id=0, has_side_effects=True, vmem_limit_bytes=50 * 1024 * 1024
        ),
        name="mixer",
    )(sig, gate, b_in, c_out, dt, rate, skip, ngain, resid, info)


def swap_blocks(v, lanes):
    n = v.shape[0]
    v = v.reshape(n // 2, 2, 8, 256)
    left = iota((n // 2, 8, 128), 2) < 64
    out = []
    for hf in range(2):
        v0 = v[:, 0, :, hf * 128 : hf * 128 + 128]
        v1 = v[:, 1, :, hf * 128 : hf * 128 + 128]
        r0 = pltpu.roll(v0, 64, 2)
        r1 = pltpu.roll(v1, 64, 2)
        u0 = jnp.where(left, v0, r1)
        u1 = jnp.where(left, r0, v1)
        out.append(jnp.concatenate([u0, u1], axis=1).astype(BF16))
    return out


def expert_kernel(w, tok, infos, part_a, part_b, xall, oh, wcol, rbuf, r2, oall):
    e = pl.program_id(0)

    @pl.when(e == 0)
    def _():
        upper = (iota((CH, CH), 0) < iota((CH, CH), 1)).astype(F32)
        who = iota((HALF, CH), 0).astype(F32)
        for b in range(2):
            r0, r1 = infos[b, 0:1, :], infos[b, 1:2, :]
            w0, w1 = infos[b, 2:3, :], infos[b, 3:4, :]
            m = jnp.where(r0 == who, 1.0, jnp.where(r1 == who, 1.0, 0.0))
            place = dot(m, upper, 1, 0)
            share = jnp.where(r0 == who, w0, jnp.where(r1 == who, w1, 0.0))
            slot = iota((SLOT, CH), 0).astype(F32)
            for k in range(HALF):
                hit = jnp.where(slot == place[k : k + 1, :], m[k : k + 1, :], 0.0)
                oh[b, k * SLOT : (k + 1) * SLOT, :] = hit.astype(BF16)
                ws = jnp.sum(hit * share[k : k + 1, :], axis=1, keepdims=True)
                wcol[k, b * SLOT : (b + 1) * SLOT, :] = jnp.broadcast_to(ws, (SLOT, 256))

        def gather(src, _):
            for b in range(2):
                x = dot(oh[b], tok[b, src], 1, 0).astype(BF16)
                xall[:, src, b * SLOT : (b + 1) * SLOT, :] = x.reshape(HALF, SLOT, WID)
            return 0

        lax.fori_loop(0, 16, gather, 0)

    def stage1(g, _):
        x = jnp.concatenate(
            [xall[e, 2 * g, :, 0:256], xall[e, 2 * g, :, 256:512],
             xall[e, 2 * g + 1, :, 0:256], xall[e, 2 * g + 1, :, 256:512]], axis=0
        )
        mid = dot(w[0, 0:512, :], x, 1, 1)
        for hf, u in enumerate(swap_blocks(mid.reshape(64, 8, 256), None)):
            u = u.reshape(2, 8, 2, 16, 128)
            rows = pl.ds(pl.multiple_of((2 * g + hf) * 16, 16), 16)
            rbuf[:, :, rows, 0:128] = u[:, :, 0]
            rbuf[:, :, rows, 128:256] = u[:, :, 1]
        return 0

    lax.fori_loop(0, 8, stage1, 0)

    def stage2(g, _):
        up = dot(w[0, 512:1280, :], rbuf[0, g], 1, 0)
        gt = dot(w[0, 1280:2048, :], rbuf[1, g], 1, 0)
        h = (silu(gt) * up).astype(BF16)
        wd = jnp.concatenate([w[0, 2048:2304, :], w[0, 2304:2560, :], w[0, 2560:2816, :]], axis=1)
        mid = dot(wd, h, 1, 0)
        for hf, u in enumerate(swap_blocks(mid.reshape(32, 8, 256), None)):
            u = u.reshape(8, 2, 16, 128)
            rows = pl.ds(pl.multiple_of((2 * g + hf) * 16, 16), 16)
            r2[:, rows, 0:128] = u[:, 0]
            r2[:, rows, 128:256] = u[:, 1]
        return 0

    lax.fori_loop(0, 8, stage2, 0)
    wc = wcol[e]
    wc = jnp.concatenate([wc, wc, wc, wc], axis=0)

    def stage3(g, _):
        o = (dot(r2[g], w[0, 2816:3072, :], 0, 0) * wc).astype(BF16).reshape(4, 2, SLOT, 256)
        rows = pl.ds(pl.multiple_of(e * SLOT, SLOT), SLOT)
        for q in range(4):
            cols = pl.ds(pl.multiple_of((4 * g + q) * 256, 256), 256)
            for b in range(2):
                oall[b, rows, cols] = o[q, b]
        return 0

    lax.fori_loop(0, 8, stage3, 0)

    @pl.when(e == HALF - 1)
    def _():
        def combine(t, _):
            cols = pl.ds(pl.multiple_of(t * 512, 512), 512)
            part_a[:, cols] = dot(oh[0], oall[0, :, cols], 0, 0)
            part_b[:, cols] = dot(oh[1], oall[1, :, cols], 0, 0).astype(BF16)
            return 0

        lax.fori_loop(0, 16, combine, 0)


def run_experts(w, tok, infos):
    vm = pl.BlockSpec(memory_space=pltpu.VMEM)
    return pl.pallas_call(
        expert_kernel,
        grid=(HALF,),
        out_shape=(jax.ShapeDtypeStruct((CH, 8192), F32), jax.ShapeDtypeStruct((CH, 8192), BF16)),
        in_specs=[pl.BlockSpec((1, PACK, 256), lambda e: (e, 0, 0)), vm, vm],
        out_specs=(vm, vm),
        scratch_shapes=[
            pltpu.VMEM((HALF, 16, 64, WID), BF16),
            pltpu.VMEM((2, 256, CH), BF16),
            pltpu.VMEM((HALF, 64, 256), F32),
            pltpu.VMEM((2, 8, 256, 256), BF16),
            pltpu.VMEM((8, 256, 256), BF16),
            pltpu.VMEM((2, 256, 8192), BF16),
        ],
        compiler_params=pltpu.CompilerParams(vmem_limit_bytes=56 * 1024 * 1024),
        name="experts",
    )(w, tok, infos)


def body(
    signal, out_gate, state_in, state_out, step_size, head_log_decay, skip_gain, norm_gain, residual,
    route, combine_weight, up_first, up_second, gate_first, gate_second, down_first, down_second,
):
    packed = jnp.concatenate(
        [up_second[0].T, gate_second[0].T, up_first[0].T, gate_first[0].T,
         down_second[0, 0:256].T, down_second[0, 256:512].T, down_second[0, 512:768].T, down_first[0]],
        axis=0,
    )
    core = lax.rem(lax.axis_index("seq"), 2)
    j = lax.axis_index("exp")
    part = jnp.where(core == j // HALF, 0, 1)
    mine = lax.dynamic_slice(packed, (part * (PACK // 2), 0), (PACK // 2, 256))
    perm = []
    for y in range(4):
        for c in range(2):
            for s in range(16):
                h = s // HALF
                p = 0 if c == h else 1
                perm.append(((y * 2 + c) * 16 + s, (y * 2 + h) * 16 + 2 * (s - HALF * h) + p))
    mine = lax.ppermute(mine, ("seq", "exp"), perm)
    weights = lax.all_gather(mine, "exp").reshape(HALF, PACK, 256)

    info = jnp.concatenate([route.T.astype(F32), combine_weight, jnp.zeros((4, CH), F32)], axis=0)
    skip = jnp.tile(skip_gain, 16).reshape(1, CH) * (jnp.arange(CH) < 8).astype(F32)[None]
    mixed, tok, infos = run_mixer(
        signal, out_gate, state_in, state_out, step_size, head_log_decay, skip,
        norm_gain.reshape(1, WID), residual, info,
    )
    mine_part, other = run_experts(weights, tok, infos)
    got = lax.ppermute(other, "seq", [(s, s ^ 1) for s in range(8)])
    routed = (mine_part + got.astype(F32)).astype(BF16)
    return mixed, routed


def solution(mesh):
    in_specs = (
        P("seq", "exp"), P("seq", "exp"), P("seq", None), P("seq", None), P("exp", "seq"), P("exp", "seq"),
        P("exp"), P("exp"), P("seq", "exp"), P(("seq", "exp"), None), P(None, ("seq", "exp")),
        P("exp", None, None), P("exp", None, None), P("exp", None, None), P("exp", None, None),
        P("exp", None, None), P("exp", None, None),
    )
    out_specs = (P("seq", "exp"), P(("seq", "exp"), None))
    return jax.shard_map(body, mesh=mesh, in_specs=in_specs, out_specs=out_specs, check_vma=False)
```

```python
import jax
import jax.numpy as jnp
from jax import lax
from jax.experimental import pallas as pl
from jax.experimental.pallas import tpu as pltpu
from jax.sharding import PartitionSpec as P

MESH = pl.DeviceIdType.MESH
HIGH = lax.Precision.HIGHEST
EPS = 1e-05
F32, BF16 = jnp.float32, jnp.bfloat16
CH = 128
NCH = 16
WID = 512
SLOT = 32
HALF = 8
PACK = 3072


def iota(shape, dim):
    return lax.broadcasted_iota(jnp.int32, shape, dim)


def dot(a, b, ca, cb, precision=None):
    return lax.dot_general(
        a, b, (((ca,), (cb,)), ((), ())), precision=precision, preferred_element_type=F32
    )


def halves(v):
    hi = v.astype(BF16)
    return hi, (v - hi.astype(F32)).astype(BF16)


def rcopy(src, dst, send, recv, dev):
    return pltpu.make_async_remote_copy(
        src_ref=src, dst_ref=dst, send_sem=send, recv_sem=recv, device_id=dev, device_id_type=MESH
    )


def silu(v):
    return v * (0.5 + 0.5 * jnp.tanh(0.5 * v))


THIRD, PART = 1024, 512
U1, U2, U3 = 4, 4, 4


def swap_blocks(v):
    n = v.shape[0]
    v = v.reshape(n // 2, 2, 8, 256)
    left = iota((n // 2, 8, 128), 2) < 64
    out = []
    for hf in range(2):
        v0 = v[:, 0, :, hf * 128 : hf * 128 + 128]
        v1 = v[:, 1, :, hf * 128 : hf * 128 + 128]
        u0 = jnp.where(left, v0, pltpu.roll(v1, 64, 2))
        u1 = jnp.where(left, pltpu.roll(v0, 64, 2), v1)
        out.append(jnp.concatenate([u0, u1], axis=1).astype(BF16))
    return out


class Weights:
    def __init__(self, me_e, me_s, pk, wbuf, send, f_sem, b_sem, y_sem, own_sem):
        self.core = lax.rem(me_s, 2)
        self.z, self.x = me_e // 4, lax.rem(me_e, 4)
        self.row = lax.rem(self.z + 4 - 2 * self.core, 4)
        self.odd = lax.rem(me_s // 2, 2)
        self.me_s = me_s
        self.pk, self.wbuf, self.send = pk, wbuf, send
        self.f_sem, self.b_sem, self.y_sem, self.own_sem = f_sem, b_sem, y_sem, own_sem
        self.f_row = pl.multiple_of(self.odd * 2 * THIRD, THIRD)
        self.y_row = pl.multiple_of((1 - self.odd) * 2 * THIRD, THIRD)
        self.own = self.row * 4 + self.x
        self.is_src = self.row < 2
        self.sent = []

    def to(self, axis, step):
        if axis == "x":
            return {"exp": self.z * 4 + lax.rem(self.x + 4 + step, 4)}
        if axis == "z":
            return {"exp": lax.rem(self.z + 4 + step, 4) * 4 + self.x}
        return {"seq": lax.rem(self.me_s + 8 + 2 * step, 8)}

    def valid(self, dz, dx):
        r = lax.rem(self.row + 4 - dz, 4)
        return r < 2, lax.rem(r, 2) * 4 + lax.rem(self.x + 4 - dx, 4)

    def rows(self, tree, half):
        base = self.f_row if tree == "f" else THIRD
        n = THIRD if half is None else PART
        return pl.ds(base if half in (None, 0) else base + PART, n)

    def push(self, ok, k, tree, half, axis, step, from_own=False):
        number = len(self.sent)

        def make():
            rows = self.rows(tree, half)
            src = self.pk.at[rows] if from_own else self.wbuf.at[k, rows]
            sem = {"f": self.f_sem, "b": self.b_sem}[tree] if axis != "y" else self.y_sem
            return rcopy(src, self.wbuf.at[k, rows], self.send.at[number], sem.at[k, half or 0], self.to(axis, step))

        make().start()
        self.sent.append((ok, make))

    def start(self):
        @pl.when(self.is_src)
        def _():
            self.own_copy().start()
            for tree, axes in (("f", "xz"), ("b", "zx")):
                self.push(self.is_src, self.own, tree, None, axes[0], 1, True)
                self.push(self.is_src, self.own, tree, None, axes[0], -1, True)
            for tree, axis in (("f", "z"), ("b", "x")):
                self.push(self.is_src, self.own, tree, None, axis, 1, True)
                self.push(self.is_src, self.own, tree, None, axis, -1, True)

    def own_copy(self):
        return pltpu.make_async_copy(self.pk, self.wbuf.at[lax.rem(self.own, 8)], self.own_sem)

    def service(self, tree, first, second):
        dz, dx = (second, first) if tree == "f" else (first, second)
        ax1, ax2 = ("x", "z") if tree == "f" else ("z", "x")
        ok, k = self.valid(dz, dx)
        sem = self.f_sem if tree == "f" else self.b_sem

        @pl.when(ok)
        def _():
            two = second == 2 or (second == 0 and first == 2)
            for half in (0, 1) if two else (None,):
                ref = self.wbuf.at[k, self.rows(tree, half)]
                rcopy(ref, ref, self.send.at[0], sem.at[k, half or 0], self.to("x", 1)).wait_recv()
            if second == 0:
                if first == 1:
                    self.push(ok, k, tree, 0, ax1, 1)
                if first == 3:
                    self.push(ok, k, tree, 1, ax1, -1)
                self.push(ok, k, tree, None, ax2, 1)
                self.push(ok, k, tree, None, ax2, -1)
            if second == 1:
                self.push(ok, k, tree, 0, ax2, 1)
            if second == 3:
                self.push(ok, k, tree, 1, ax2, -1)
            if tree == "f":
                self.push(ok, k, tree, 0, "y", 1)
                self.push(ok, k, tree, 1, "y", -1)

    def wait_y(self, k):
        @pl.when(jnp.logical_or(k != self.own, jnp.logical_not(self.is_src)))
        def _():
            for half in range(2):
                ref = self.wbuf.at[k, pl.ds(self.y_row + half * PART, PART)]
                rcopy(ref, ref, self.send.at[0], self.y_sem.at[k, half], self.to("y", 1)).wait_recv()

    def drain(self):
        for ok, make in self.sent:
            @pl.when(ok)
            def _(make=make):
                make().wait_send()


LEVELS = (
    (("f", 1, 0), ("b", 1, 0), ("f", 3, 0), ("b", 3, 0)),
    (("f", 2, 0), ("b", 2, 0), ("f", 0, 1), ("f", 0, 3), ("b", 0, 1), ("b", 0, 3)),
    (("f", 1, 1), ("f", 1, 3), ("f", 3, 1), ("f", 3, 3), ("b", 1, 1), ("b", 1, 3), ("b", 3, 1), ("b", 3, 3),
     ("f", 2, 1), ("f", 2, 3), ("b", 2, 1), ("b", 2, 3)),
    (("f", 0, 2), ("b", 0, 2), ("f", 1, 2), ("f", 3, 2), ("b", 1, 2), ("b", 3, 2), ("f", 2, 2), ("b", 2, 2)),
)


def kernel(
    sig_h, gate_h, b_in, c_out, dt, rate, skip, ngain, resid_h, info, pk,
    mixed_h, routed_h,
    sig, big, sraw, amat, bmat, gtot, gend, gmid, st_loc, st_buf, ssq, land, inv_s, info_l,
    tok, xall, oh, wcol, rbuf, r2, hbuf, wbuf, other, theirs, result,
    ld_s, st_s, st_r, sq_s, sq_r, tk_s, tk_r, nb_s, nb_r, in_s, in_r,
    w_s, f_r, b_r, y_r, own_s, mx_s, pa_s, pa_r, ro_s,
):
    me_e, me_s = lax.axis_index("exp"), lax.axis_index("seq")
    core = lax.rem(me_s, 2)
    sib = me_s + 1 - 2 * core
    gate, resid, bx, sendb = (big.at[i * 2048 : (i + 1) * 2048] for i in range(4))
    loads = [
        pltpu.make_async_copy(sig_h, sig, ld_s.at[0]),
        pltpu.make_async_copy(gate_h, gate, ld_s.at[1]),
        pltpu.make_async_copy(resid_h, resid, ld_s.at[2]),
    ]
    for cp in loads:
        cp.start()

    barrier = pltpu.get_barrier_semaphore()
    for d in range(1, 16):
        pl.semaphore_signal(barrier, inc=1, device_id={"exp": lax.rem(me_e + d, 16)}, device_id_type=MESH)
    for d in range(1, 8):
        pl.semaphore_signal(barrier, inc=1, device_id={"seq": lax.rem(me_s + d, 8)}, device_id_type=MESH)
    pl.semaphore_wait(barrier, 22)
    info_cp = rcopy(info, info_l, in_s, in_r, {"seq": sib})
    info_cp.start()
    weights = Weights(me_e, me_s, pk, wbuf, w_s, f_r, b_r, y_r, own_s)
    weights.start()

    def serve(level):
        for unit in LEVELS[level]:
            weights.service(*unit)

    rate2 = jnp.concatenate([rate[:, c * CH : (c + 1) * CH] for c in range(NCH)], axis=0)
    dt2 = jnp.concatenate([dt[:, c * CH : (c + 1) * CH] for c in range(NCH)], axis=0)
    tri = (iota((CH, CH), 0) >= iota((CH, CH), 1)).astype(F32)
    run = dot(tri, rate2, 1, 1, HIGH)
    mid, end = run[63:64, :], run[127:128, :]
    av = jnp.exp(mid - run)
    bv = jnp.exp(run - mid) * dt2.T
    ah, al = halves(av)
    bh, bl = halves(bv)
    amat[:, :CH], amat[:, CH:] = ah, al
    bmat[:, :CH], bmat[:, CH:] = bh, bl
    spread = ((iota((CH, WID), 0) & 7) == (iota((CH, WID), 1) >> 6)).astype(F32)
    own = (iota((NCH, CH), 1) >> 3) == iota((NCH, CH), 0)

    def rows_of(v):
        return dot(jnp.where(own, v, 0.0), spread, 1, 0, HIGH)

    gtot[...] = rows_of(jnp.exp(-end))
    gend[...] = rows_of(jnp.exp(mid - end))
    gmid[...] = rows_of(jnp.exp(-mid))
    all_end = dot(jnp.broadcast_to(end, (8, CH)), spread, 1, 0, HIGH)

    def picker(c):
        return ((iota((2 * CH, WID), 0) & (CH - 1)) == c * 8 + (iota((2 * CH, WID), 1) >> 6)).astype(BF16)

    loads[0].wait()

    def first(c, state):
        rows = pl.ds(pl.multiple_of(c * CH, CH), CH)
        x = (dot(bmat[...], picker(c), 1, 0) * sig[rows, :]).astype(BF16)
        bx[rows, :] = x
        s = dot(b_in[rows, :].astype(BF16), x, 0, 0)
        sraw[c] = s
        return gtot[pl.ds(c, 1), :] * state + gend[pl.ds(c, 1), :] * s

    state = lax.fori_loop(0, NCH, first, jnp.zeros((16, WID), F32), unroll=U1)
    st_loc[0:16, :] = state
    st_loc[16:24, :] = jnp.exp(-all_end)
    st_buf[me_s] = st_loc[...]
    st_cp = []
    for d in range(1, 8):
        to = lax.rem(me_s + d, 8)
        st_cp.append(rcopy(st_loc, st_buf.at[me_s], st_s.at[d], st_r.at[me_s], {"seq": to}))
        st_cp[-1].start()
    loads[1].wait()
    loads[2].wait()
    serve(0)
    for d in range(1, 8):
        frm = lax.rem(me_s + 8 - d, 8)
        rcopy(st_loc, st_buf.at[frm], st_s.at[d], st_r.at[frm], {"seq": frm}).wait_recv()

    state = jnp.zeros((16, WID), F32)
    for k in range(7):
        new = st_buf[k, 16:17, :] * state + st_buf[k, 0:16, :]
        state = jnp.where(k < me_s, new, state)

    low = iota((CH, CH), 0) >= iota((CH, CH), 1)
    skip_e = dot(jnp.broadcast_to(skip[...], (8, CH)), spread, 1, 0, HIGH)[0:1, :]
    ones = jnp.ones((8, WID), BF16)

    def second(c, state):
        rows = pl.ds(pl.multiple_of(c * CH, CH), CH)
        cm = c_out[rows, :].astype(BF16)
        scores = jnp.where(low, dot(cm, b_in[rows, :].astype(BF16), 1, 1), 0.0).astype(BF16)
        enter = (gmid[pl.ds(c, 1), :] * state).astype(BF16)
        y = dot(scores, bx[rows, :], 1, 0) + dot(cm, enter, 1, 0)
        y = y * dot(amat[...], picker(c), 1, 0) + skip_e * sig[rows, :]
        g = y * silu(gate[rows, :].astype(F32))
        sig[rows, :] = g
        ssq[me_e, pl.ds(c, 1), :] = dot(ones, (g * g).astype(BF16), 1, 1)[0:1, :]
        return gtot[pl.ds(c, 1), :] * state + gend[pl.ds(c, 1), :] * sraw[c]

    lax.fori_loop(0, NCH, second, state, unroll=U2)

    sq_cp = []
    for d in range(1, 16):
        to = lax.rem(me_e + d, 16)
        sq_cp.append(rcopy(ssq.at[me_e], ssq.at[me_e], sq_s.at[d], sq_r.at[me_e], {"exp": to}))
        sq_cp[-1].start()
    serve(1)
    for d in range(1, 16):
        frm = lax.rem(me_e + 16 - d, 16)
        rcopy(ssq.at[frm], ssq.at[frm], sq_s.at[d], sq_r.at[frm], {"exp": frm}).wait_recv()
    total = ssq[0]
    for k in range(1, 16):
        total = total + ssq[k]
    inv = lax.rsqrt(total * (1.0 / 8192.0) + EPS)
    inv_t = jnp.concatenate([inv, jnp.zeros((CH - NCH, CH), F32)], axis=0).T
    ih, il = halves(inv_t)
    inv_s[:, :CH], inv_s[:, CH:] = ih, il

    def third(c):
        rows = pl.ds(pl.multiple_of(c * CH, CH), CH)
        sel = ((iota((2 * CH, WID), 0) & (CH - 1)) == c).astype(BF16)
        m = (sig[rows, :] * dot(inv_s[...], sel, 1, 0) * ngain[...]).astype(BF16)
        xall[rows, :] = m
        return (resid[rows, :].astype(F32) + m.astype(F32)).astype(BF16)

    def token_copy(c):
        rows = pl.ds(pl.multiple_of(c * CH, CH), CH)
        return rcopy(sendb.at[rows], land.at[me_e], tk_s.at[c], tk_r.at[me_e], {"exp": c})

    def send_block(k, _):
        c = lax.rem(me_e + 1 + k, 16)
        sendb[pl.ds(pl.multiple_of(c * CH, CH), CH), :] = third(c)
        token_copy(c).start()
        return 0

    lax.fori_loop(0, 15, send_block, 0, unroll=U3)
    land[me_e] = third(me_e)
    mixed_cp = pltpu.make_async_copy(xall.at[0:2048], mixed_h, mx_s)
    mixed_cp.start()

    info_cp.wait()
    shift = (core * HALF).astype(F32)
    upper = (iota((CH, CH), 0) < iota((CH, CH), 1)).astype(F32)
    who = iota((HALF, CH), 0).astype(F32) + shift
    slot = iota((SLOT, CH), 0).astype(F32)
    for b, ref in enumerate((info, info_l)):
        r0, r1, w0, w1 = (ref[i : i + 1, :] for i in range(4))
        m = jnp.where(r0 == who, 1.0, jnp.where(r1 == who, 1.0, 0.0))
        place = dot(m, upper, 1, 0)
        share = jnp.where(r0 == who, w0, jnp.where(r1 == who, w1, 0.0))
        for k in range(HALF):
            hit = jnp.where(slot == place[k : k + 1, :], m[k : k + 1, :], 0.0)
            oh[b, k * SLOT : (k + 1) * SLOT, :] = hit.astype(BF16)
            ws = jnp.sum(hit * share[k : k + 1, :], axis=1, keepdims=True)
            wcol[k, b * SLOT : (b + 1) * SLOT, :] = jnp.broadcast_to(ws, (SLOT, 256))

    serve(2)

    def squares(src):
        v = land[src].astype(F32)
        v = v * v
        return v[:, 0:128] + v[:, 128:256] + v[:, 256:384] + v[:, 384:512]

    def arrive(k, acc):
        src = lax.rem(me_e + 15 - k, 16)
        rcopy(land.at[src], land.at[src], tk_s.at[src], tk_r.at[src], {"exp": src}).wait_recv()
        return acc + squares(src)

    acc = lax.fori_loop(0, 15, arrive, squares(me_e))
    rs = lax.rsqrt(jnp.sum(acc, axis=1, keepdims=True) * (1.0 / 8192.0) + EPS)

    def near(src):
        return rcopy(tok.at[0, src], tok.at[1, src], nb_s.at[src], nb_r.at[src], {"seq": sib})

    def normal(src, _):
        tok[0, src] = (land[src].astype(F32) * rs).astype(BF16)
        near(src).start()
        return 0

    lax.fori_loop(0, 16, normal, 0, unroll=2)
    mixed_cp.wait()

    def gather(b):
        def one(src, _):
            x = dot(oh[b], tok[b, src], 1, 0).astype(BF16)
            for k in range(HALF):
                rows = pl.ds(pl.multiple_of(k * 1024 + src * 64 + b * SLOT, SLOT), SLOT)
                xall[rows, :] = x[k * SLOT : (k + 1) * SLOT]
            return 0

        return one

    lax.fori_loop(0, 16, gather(0), 0, unroll=4)
    serve(3)

    @pl.when(weights.is_src)
    def _():
        weights.own_copy().wait()

    def settle(src, _):
        near(src).wait()
        return 0

    lax.fori_loop(0, 16, settle, 0)
    lax.fori_loop(0, 16, gather(1), 0, unroll=4)

    def sent(k, _):
        token_copy(lax.rem(me_e + 1 + k, 16)).wait_send()
        return 0

    lax.fori_loop(0, 15, sent, 0)

    def expert(step, _):
        e = lax.rem(step + weights.own, 8)
        weights.wait_y(e)
        for g in range(8):
            base = e * 1024 + g * 128
            x0 = xall[pl.ds(pl.multiple_of(base, 64), 64), :]
            x1 = xall[pl.ds(pl.multiple_of(base + 64, 64), 64), :]
            x = jnp.concatenate([x0[:, 0:256], x0[:, 256:512], x1[:, 0:256], x1[:, 256:512]], axis=0)
            for m in range(2):
                mid = dot(wbuf[e, m * 256 : m * 256 + 256, :], x, 1, 1)
                for hf, u in enumerate(swap_blocks(mid.reshape(32, 8, 256))):
                    u = u.reshape(8, 2, 16, 128)
                    rows = pl.ds((2 * g + hf) * 16, 16)
                    rbuf[m, :, rows, 0:128] = u[:, 0]
                    rbuf[m, :, rows, 128:256] = u[:, 1]
        for g in range(8):
            for t in range(3):
                up = dot(wbuf[e, 512 + t * 256 : 768 + t * 256, :], rbuf[0, g], 1, 0)
                gt = dot(wbuf[e, 1280 + t * 256 : 1536 + t * 256, :], rbuf[1, g], 1, 0)
                hbuf[g, t * 256 : t * 256 + 256, :] = (silu(gt) * up).astype(BF16)
        for g in range(8):
            mid = sum(
                dot(wbuf[e, 2048 + t * 256 : 2304 + t * 256, :], hbuf[g, t * 256 : t * 256 + 256, :], 1, 0)
                for t in range(3)
            )
            for hf, u in enumerate(swap_blocks(mid.reshape(32, 8, 256))):
                u = u.reshape(8, 2, 16, 128)
                rows = pl.ds((2 * g + hf) * 16, 16)
                r2[:, rows, 0:128] = u[:, 0]
                r2[:, rows, 128:256] = u[:, 1]
        wc = wcol[e]
        wc = jnp.concatenate([wc, wc, wc, wc], axis=0)
        for g in range(8):
            o = (dot(r2[g], wbuf[e, 2816:3072, :], 0, 0) * wc).astype(BF16).reshape(4, 2, SLOT, 256)
            for q in range(4):
                for b in range(2):
                    rows = pl.ds(pl.multiple_of(e * SLOT + ((2 * g + q // 2) * 2 + b) * 256, SLOT), SLOT)
                    big[rows, (q % 2) * 256 : (q % 2) * 256 + 256] = o[q, b]
        return 0

    lax.fori_loop(0, HALF, expert, 0)

    def part(t, b):
        return dot(oh[b], big[pl.ds(pl.multiple_of((2 * t + b) * 256, 256), 256), :], 0, 0)

    def part_copy(t):
        return rcopy(other.at[t], theirs.at[t], pa_s.at[t], pa_r.at[t], {"seq": sib})

    def out_copy(t):
        cols = pl.ds(pl.multiple_of(t * 512, 512), 512)
        return pltpu.make_async_copy(result.at[t], routed_h.at[:, cols], ro_s.at[t])

    def give(t, _):
        other[t] = part(t, 1).astype(BF16)
        part_copy(t).start()
        return 0

    lax.fori_loop(0, 16, give, 0, unroll=2)

    def take(t, _):
        mine = part(t, 0)
        part_copy(t).wait()
        result[t] = (mine + theirs[t].astype(F32)).astype(BF16)
        out_copy(t).start()
        return 0

    lax.fori_loop(0, 16, take, 0, unroll=2)

    def done(t, _):
        out_copy(t).wait()
        return 0

    lax.fori_loop(0, 16, done, 0)
    for cp in st_cp + sq_cp:
        cp.wait_send()
    weights.drain()


def run(*operands):
    vm = pl.BlockSpec(memory_space=pltpu.VMEM)
    hbm = pl.BlockSpec(memory_space=pl.ANY)
    dma = pltpu.SemaphoreType.DMA
    return pl.pallas_call(
        kernel,
        out_shape=(jax.ShapeDtypeStruct((2048, WID), BF16), jax.ShapeDtypeStruct((CH, 8192), BF16)),
        in_specs=[hbm, hbm, vm, vm, vm, vm, vm, vm, hbm, vm, hbm],
        out_specs=(hbm, hbm),
        scratch_shapes=[
            pltpu.VMEM((2048, WID), F32),
            pltpu.VMEM((8192, WID), BF16),
            pltpu.VMEM((NCH, 16, WID), F32),
            pltpu.VMEM((CH, 2 * CH), BF16),
            pltpu.VMEM((CH, 2 * CH), BF16),
            pltpu.VMEM((NCH, WID), F32),
            pltpu.VMEM((NCH, WID), F32),
            pltpu.VMEM((NCH, WID), F32),
            pltpu.VMEM((24, WID), F32),
            pltpu.VMEM((8, 24, WID), F32),
            pltpu.VMEM((16, NCH, CH), F32),
            pltpu.VMEM((16, CH, WID), BF16),
            pltpu.VMEM((CH, 2 * CH), BF16),
            pltpu.VMEM((8, CH), F32),
            pltpu.VMEM((2, 16, CH, WID), BF16),
            pltpu.VMEM((8192, WID), BF16),
            pltpu.VMEM((2, 256, CH), BF16),
            pltpu.VMEM((HALF, 64, 256), F32),
            pltpu.VMEM((2, 8, 256, 256), BF16),
            pltpu.VMEM((8, 256, 256), BF16),
            pltpu.VMEM((8, 768, 256), BF16),
            pltpu.VMEM((HALF, PACK, 256), BF16),
            pltpu.VMEM((16, CH, WID), BF16),
            pltpu.VMEM((16, CH, WID), BF16),
            pltpu.VMEM((16, CH, WID), BF16),
            dma((3,)), dma((8,)), dma((8,)), dma((16,)), dma((16,)), dma((16,)), dma((16,)), dma((16,)), dma((16,)),
            dma, dma,
            dma((96,)), dma((8, 2)), dma((8, 2)), dma((8, 2)), dma, dma, dma((16,)), dma((16,)), dma((16,)),
        ],
        compiler_params=pltpu.CompilerParams(
            collective_id=0, has_side_effects=True, vmem_limit_bytes=61 * 1024 * 1024
        ),
        name="mixer_experts",
    )(*operands)


def body(
    signal, out_gate, state_in, state_out, step_size, head_log_decay, skip_gain, norm_gain, residual,
    route, combine_weight, up_first, up_second, gate_first, gate_second, down_first, down_second,
):
    packed = jnp.concatenate(
        [up_second[0].T, gate_second[0].T, up_first[0].T, gate_first[0].T,
         down_second[0, 0:256].T, down_second[0, 256:512].T, down_second[0, 512:768].T, down_first[0]],
        axis=0,
    )
    info = jnp.concatenate([route.T.astype(F32), combine_weight, jnp.zeros((4, CH), F32)], axis=0)
    skip = jnp.tile(skip_gain, 16).reshape(1, CH) * (jnp.arange(CH) < 8).astype(F32)[None]
    return run(
        signal, out_gate, state_in, state_out, step_size, head_log_decay, skip,
        norm_gain.reshape(1, WID), residual, info, packed,
    )


def solution(mesh):
    in_specs = (
        P("seq", "exp"), P("seq", "exp"), P("seq", None), P("seq", None), P("exp", "seq"), P("exp", "seq"),
        P("exp"), P("exp"), P("seq", "exp"), P(("seq", "exp"), None), P(None, ("seq", "exp")),
        P("exp", None, None), P("exp", None, None), P("exp", None, None), P("exp", None, None),
        P("exp", None, None), P("exp", None, None),
    )
    out_specs = (P("seq", "exp"), P(("seq", "exp"), None))
    return jax.shard_map(body, mesh=mesh, in_specs=in_specs, out_specs=out_specs, check_vma=False)
```

```python
import jax
import jax.numpy as jnp
from jax import lax
from jax.experimental import pallas as pl
from jax.experimental.pallas import tpu as pltpu
from jax.sharding import PartitionSpec as P

MESH = pl.DeviceIdType.MESH
HIGH = lax.Precision.HIGHEST
EPS = 1e-05
F32, BF16 = jnp.float32, jnp.bfloat16
CH = 128
NCH = 16
WID = 512
SLOT = 32
HALF = 8
PACK = 3072


def iota(shape, dim):
    return lax.broadcasted_iota(jnp.int32, shape, dim)


def dot(a, b, ca, cb, precision=None):
    return lax.dot_general(
        a, b, (((ca,), (cb,)), ((), ())), precision=precision, preferred_element_type=F32
    )


def halves(v):
    hi = v.astype(BF16)
    return hi, (v - hi.astype(F32)).astype(BF16)


def rcopy(src, dst, send, recv, dev):
    return pltpu.make_async_remote_copy(
        src_ref=src, dst_ref=dst, send_sem=send, recv_sem=recv, device_id=dev, device_id_type=MESH
    )


def silu(v):
    return v * (0.5 + 0.5 * jnp.tanh(0.5 * v))


NF = 768
NY = PACK - 3 * NF
FAR = ((2, 2), (1, 2), (2, 1), (2, 3), (3, 2), (1, 1), (3, 3), (1, 3), (3, 1), (0, 2), (2, 0), (0, 1), (0, 3), (1, 0), (3, 0))
U1, U2 = 8, 8


def swap_blocks(v):
    n = v.shape[0]
    v = v.reshape(n // 2, 2, 8, 256)
    left = iota((n // 2, 8, 128), 2) < 64
    out = []
    for hf in range(2):
        v0 = v[:, 0, :, hf * 128 : hf * 128 + 128]
        v1 = v[:, 1, :, hf * 128 : hf * 128 + 128]
        u0 = jnp.where(left, v0, pltpu.roll(v1, 64, 2))
        u1 = jnp.where(left, pltpu.roll(v0, 64, 2), v1)
        out.append(jnp.concatenate([u0, u1], axis=1).astype(BF16))
    return out


class Weights:
    def __init__(self, me_e, me_s, wbuf, send, f_sem, b_sem, y_sem):
        self.core = lax.rem(me_s, 2)
        self.z, self.x = me_e // 4, lax.rem(me_e, 4)
        self.row = lax.rem(self.z + 4 - 2 * self.core, 4)
        self.odd = lax.rem(me_s // 2, 2)
        self.me_s = me_s
        self.wbuf, self.send = wbuf, send
        self.f_sem, self.b_sem, self.y_sem = f_sem, b_sem, y_sem
        self.own = lax.rem(self.row, 2) * 4 + self.x
        self.near_row = (self.row == 1) | (self.row == 2)
        self.is_src = self.row < 2
        self.sent = []
        self.known = {(dz, dx): self.valid(dz, dx) for dz in range(4) for dx in range(4)}

    def to(self, axis, step):
        if axis == "x":
            return {"exp": self.z * 4 + lax.rem(self.x + 4 + step, 4)}
        if axis == "z":
            return {"exp": lax.rem(self.z + 4 + step, 4) * 4 + self.x}
        return {"seq": lax.rem(self.me_s + 8 + 2 * step, 8)}

    def valid(self, dz, dx):
        r = lax.rem(self.row + 4 - dz, 4)
        return r < 2, lax.rem(r, 2) * 4 + lax.rem(self.x + 4 - dx, 4)

    def rows(self, tree, half):
        base = self.odd * (PACK - NF) if tree == "f" else NF + self.odd * (PACK - 3 * NF)
        n = NF if half is None else NF // 2
        return pl.ds(pl.multiple_of(base + (half or 0) * (NF // 2), 64), n)

    def y_rows(self, tree, half, odd):
        base, n = (odd * (PACK - NF), NF) if tree == "f" else (NF + odd * (PACK - 2 * NF - NY), NY)
        return pl.ds(pl.multiple_of(base + half * (n // 2), 64), n // 2)

    def push(self, ok, k, tree, half, axis, step):
        number = len(self.sent)

        def make():
            rows = self.y_rows(tree, half, self.odd) if axis == "y" else self.rows(tree, half)
            ref = self.wbuf.at[k, rows]
            sem = (self.f_sem if tree == "f" else self.b_sem).at[k, half or 0]
            if axis == "y":
                sem = self.y_sem.at[k, half + (0 if tree == "f" else 2)]
            return rcopy(ref, ref, self.send.at[number], sem, self.to(axis, step))

        make().start()
        self.sent.append((ok, make))

    def start(self):
        @pl.when(self.is_src)
        def _():
            for tree, axes in (("f", "xz"), ("b", "zx")):
                self.push(self.is_src, self.own, tree, None, axes[0], 1)
                self.push(self.is_src, self.own, tree, None, axes[0], -1)
            for tree, axis in (("f", "z"), ("b", "x")):
                self.push(self.is_src, self.own, tree, None, axis, 1)
                self.push(self.is_src, self.own, tree, None, axis, -1)

    def service(self, tree, first, second):
        dz, dx = (second, first) if tree == "f" else (first, second)
        ax1, ax2 = ("x", "z") if tree == "f" else ("z", "x")
        ok, k = self.known[dz, dx]
        sem = self.f_sem if tree == "f" else self.b_sem

        @pl.when(ok)
        def _():
            two = second == 2 or (second == 0 and first == 2)
            for half in (0, 1) if two else (None,):
                ref = self.wbuf.at[k, self.rows(tree, half)]
                rcopy(ref, ref, self.send.at[0], sem.at[k, half or 0], self.to("x", 1)).wait_recv()
            if second == 0:
                if first == 1:
                    self.push(ok, k, tree, 0, ax1, 1)
                if first == 3:
                    self.push(ok, k, tree, 1, ax1, -1)
                self.push(ok, k, tree, None, ax2, 1)
                self.push(ok, k, tree, None, ax2, -1)
            if second == 1:
                self.push(ok, k, tree, 0, ax2, 1)
            if second == 3:
                self.push(ok, k, tree, 1, ax2, -1)
            if tree == "f" or NY:
                self.push(ok, k, tree, 0, "y", 1)
                self.push(ok, k, tree, 1, "y", -1)

    def wait_y(self, k):
        @pl.when(jnp.logical_or(k != self.own, jnp.logical_not(self.is_src)))
        def _():
            for part in range(4 if NY else 2):
                ref = self.wbuf.at[k, self.y_rows("fb"[part // 2], part % 2, 1 - self.odd)]
                rcopy(ref, ref, self.send.at[0], self.y_sem.at[k, part], self.to("y", 1)).wait_recv()

    def drain(self):
        for ok, make in self.sent:
            @pl.when(ok)
            def _(make=make):
                make().wait_send()


SERVE = {
    "state": (("f", 1, 0), ("b", 1, 0), ("f", 3, 0), ("b", 3, 0)),
    "ssq": (("f", 2, 0), ("b", 0, 1), ("b", 0, 3), ("f", 0, 1), ("f", 0, 3), ("b", 2, 0)),
    "sent": (("f", 1, 1), ("f", 1, 3), ("f", 3, 1), ("f", 3, 3), ("b", 1, 1), ("b", 1, 3), ("b", 3, 1), ("b", 3, 3)),
    "arrived": (("f", 2, 1), ("f", 2, 3), ("b", 0, 2), ("b", 1, 2), ("b", 3, 2)),
    "near": (("b", 2, 1), ("b", 2, 3), ("f", 0, 2)),
    2: (("f", 1, 2), ("f", 3, 2), ("f", 2, 2), ("b", 2, 2)),
}


def kernel(
    sig_h, gate_h, b_in, c_out, dt, rate, skip, ngain, resid_h, route, share_in,
    uf_h, us_h, gf_h, gs_h, df_h, ds_h,
    mixed_h, routed_h,
    sig, big, sraw, amat, bmat, gtot, gend, gmid, st_loc, st_buf, ssq, land, inv_s, info, info_l, raw_f, raw_s, raw_d,
    tok, xall, oh, oht, wcol, rbuf, r2, hbuf, wbuf, other, theirs, result,
    ld_s, st_s, st_r, sq_s, sq_r, tk_s, tk_r, nb_s, nb_r, in_s, in_r,
    w_s, f_r, b_r, y_r, rw_s, mx_s, pa_s, pa_r, ro_s,
):
    me_e, me_s = lax.axis_index("exp"), lax.axis_index("seq")
    core = lax.rem(me_s, 2)
    sib = me_s + 1 - 2 * core
    gate, resid, bx, sendb = (big.at[i * 2048 : (i + 1) * 2048] for i in range(4))
    loads = [
        pltpu.make_async_copy(sig_h, sig, ld_s.at[0]),
        pltpu.make_async_copy(gate_h, gate, ld_s.at[1]),
        pltpu.make_async_copy(resid_h, resid, ld_s.at[2]),
    ]
    weights = Weights(me_e, me_s, wbuf, w_s, f_r, b_r, y_r)
    mine = wbuf.at[weights.own]
    raws = [
        pltpu.make_async_copy(us_h.at[0], raw_s.at[0], rw_s.at[0]),
        pltpu.make_async_copy(gs_h.at[0], raw_s.at[1], rw_s.at[1]),
        pltpu.make_async_copy(uf_h.at[0], raw_f.at[0], rw_s.at[2]),
        pltpu.make_async_copy(gf_h.at[0], raw_f.at[1], rw_s.at[3]),
        pltpu.make_async_copy(ds_h.at[0], raw_d, rw_s.at[4]),
        pltpu.make_async_copy(df_h.at[0], mine.at[2816:3072], rw_s.at[5]),
    ]

    @pl.when(weights.is_src)
    def _():
        for cp in raws:
            cp.start()

    for cp in loads:
        cp.start()

    barrier = pltpu.get_barrier_semaphore()
    for d in range(1, 16):
        pl.semaphore_signal(barrier, inc=1, device_id={"exp": lax.rem(me_e + d, 16)}, device_id_type=MESH)
    for d in range(1, 8):
        pl.semaphore_signal(barrier, inc=1, device_id={"seq": lax.rem(me_s + d, 8)}, device_id_type=MESH)
    info[...] = jnp.concatenate([route[...].astype(F32), share_in[...], jnp.zeros((4, CH), F32)], axis=0)

    @pl.when(weights.is_src)
    def _():
        for cp in raws:
            cp.wait()
        for i in range(2):
            mine[i * 256 : i * 256 + 256, :] = raw_s[i].T
            for t in range(3):
                mine[512 + (3 * i + t) * 256 : 768 + (3 * i + t) * 256, :] = raw_f[i, :, t * 256 : t * 256 + 256].T
        for t in range(3):
            mine[2048 + t * 256 : 2304 + t * 256, :] = raw_d[t * 256 : t * 256 + 256, :].T


    def serve(when):
        for unit in SERVE.get(when, ()):
            weights.service(*unit)

    rate2 = jnp.concatenate([rate[:, c * CH : (c + 1) * CH] for c in range(NCH)], axis=0)
    dt2 = jnp.concatenate([dt[:, c * CH : (c + 1) * CH] for c in range(NCH)], axis=0)
    tri = (iota((CH, CH), 0) >= iota((CH, CH), 1)).astype(F32)
    run = dot(tri, rate2, 1, 1, HIGH)
    mid, end = run[63:64, :], run[127:128, :]
    av = jnp.exp(mid - run)
    bv = jnp.exp(run - mid) * dt2.T
    ah, al = halves(av)
    bh, bl = halves(bv)
    amat[:, :CH], amat[:, CH:] = ah, al
    bmat[:, :CH], bmat[:, CH:] = bh, bl
    spread = ((iota((CH, WID), 0) & 7) == (iota((CH, WID), 1) >> 6)).astype(F32)
    own = (iota((NCH, CH), 1) >> 3) == iota((NCH, CH), 0)

    def rows_of(v):
        return dot(jnp.where(own, v, 0.0), spread, 1, 0, HIGH)

    gtot[...] = rows_of(jnp.exp(-end))
    gend[...] = rows_of(jnp.exp(mid - end))
    gmid[...] = rows_of(jnp.exp(-mid))
    all_end = dot(jnp.broadcast_to(end, (8, CH)), spread, 1, 0, HIGH)

    pl.semaphore_wait(barrier, 22)
    info_cp = rcopy(info, info_l, in_s, in_r, {"seq": sib})
    info_cp.start()
    weights.start()

    def picker(c):
        return ((iota((2 * CH, WID), 0) & (CH - 1)) == c * 8 + (iota((2 * CH, WID), 1) >> 6)).astype(BF16)

    loads[0].wait()

    def first(c, state):
        rows = pl.ds(pl.multiple_of(c * CH, CH), CH)
        x = (dot(bmat[...], picker(c), 1, 0) * sig[rows, :]).astype(BF16)
        bx[rows, :] = x
        s = dot(b_in[:, rows].astype(BF16), x, 1, 0)
        sraw[c] = s
        return gtot[pl.ds(c, 1), :] * state + gend[pl.ds(c, 1), :] * s

    state = lax.fori_loop(0, NCH, first, jnp.zeros((16, WID), F32), unroll=U1)
    gh, gl = halves(jnp.exp(-all_end))
    st_loc[...] = jnp.concatenate([state.astype(BF16), gh, gl], axis=0)
    st_buf[me_s] = st_loc[...]

    def state_copy(d, to):
        return rcopy(st_loc, st_buf.at[me_s], st_s.at[d], st_r.at[me_s], {"seq": to})

    for d in range(1, 8):
        @pl.when(me_s + d < 8)
        def _(d=d):
            state_copy(d, me_s + d).start()
    loads[1].wait()
    loads[2].wait()
    serve("state")
    for d in range(1, 8):
        @pl.when(me_s >= d)
        def _(d=d):
            frm = me_s - d
            rcopy(st_loc, st_buf.at[frm], st_s.at[d], st_r.at[frm], {"seq": frm}).wait_recv()

    state = jnp.zeros((16, WID), F32)
    for k in range(7):
        got = st_buf[k].astype(F32)
        state = jnp.where(k < me_s, (got[16:17] + got[24:25]) * state + got[0:16], state)

    low = iota((CH, CH), 0) >= iota((CH, CH), 1)
    skip_e = dot(jnp.broadcast_to(skip[...], (8, 8)), spread[0:8, :], 1, 0, HIGH)[0:1, :]
    ones = jnp.ones((8, WID), BF16)

    def second(c, state):
        rows = pl.ds(pl.multiple_of(c * CH, CH), CH)
        cm = c_out[:, rows].astype(BF16)
        scores = jnp.where(low, dot(cm, b_in[:, rows].astype(BF16), 0, 0), 0.0).astype(BF16)
        enter = (gmid[pl.ds(c, 1), :] * state).astype(BF16)
        y = dot(scores, bx[rows, :], 1, 0) + dot(cm, enter, 0, 0)
        y = y * dot(amat[...], picker(c), 1, 0) + skip_e * sig[rows, :]
        g = y * silu(gate[rows, :].astype(F32))
        sig[rows, :] = g
        ssq[me_e, pl.ds(c, 1), :] = dot(ones, (g * g).astype(BF16), 1, 1)[0:1, :]
        return gtot[pl.ds(c, 1), :] * state + gend[pl.ds(c, 1), :] * sraw[c]

    lax.fori_loop(0, NCH, second, state, unroll=U2)

    sq_cp = []
    for d in range(1, 16):
        to = lax.rem(me_e + d, 16)
        sq_cp.append(rcopy(ssq.at[me_e], ssq.at[me_e], sq_s.at[d], sq_r.at[me_e], {"exp": to}))
        sq_cp[-1].start()
    serve("ssq")
    for d in range(1, 16):
        frm = lax.rem(me_e + 16 - d, 16)
        rcopy(ssq.at[frm], ssq.at[frm], sq_s.at[d], sq_r.at[frm], {"exp": frm}).wait_recv()
    total = ssq[0]
    for k in range(1, 16):
        total = total + ssq[k]
    inv = lax.rsqrt(total * (1.0 / 8192.0) + EPS)
    inv_t = jnp.concatenate([inv, jnp.zeros((CH - NCH, CH), F32)], axis=0).T
    ih, il = halves(inv_t)
    inv_s[:, :CH], inv_s[:, CH:] = ih, il

    def third(c):
        rows = pl.ds(pl.multiple_of(c * CH, CH), CH)
        sel = ((iota((2 * CH, WID), 0) & (CH - 1)) == c).astype(BF16)
        m = (sig[rows, :] * dot(inv_s[...], sel, 1, 0) * ngain[...]).astype(BF16)
        xall[rows, :] = m
        return (resid[rows, :].astype(F32) + m.astype(F32)).astype(BF16)

    def token_copy(c):
        rows = pl.ds(pl.multiple_of(c * CH, CH), CH)
        return rcopy(sendb.at[rows], land.at[me_e], tk_s.at[c], tk_r.at[me_e], {"exp": c})

    def peer(dz, dx):
        return lax.rem(weights.z + dz, 4) * 4 + lax.rem(weights.x + dx, 4)

    for dz, dx in FAR:
        c = peer(dz, dx)
        sendb[pl.ds(pl.multiple_of(c * CH, CH), CH), :] = third(c)
        token_copy(c).start()
    land[me_e] = third(me_e)
    mixed_cp = pltpu.make_async_copy(xall.at[0:2048], mixed_h, mx_s)
    mixed_cp.start()

    info_cp.wait()
    shift = (core * HALF).astype(F32)
    upper = (iota((CH, CH), 0) < iota((CH, CH), 1)).astype(F32)
    who = iota((HALF, CH), 0).astype(F32) + shift
    slot = iota((SLOT, CH), 0).astype(F32)
    for b, ref in enumerate((info, info_l)):
        r0, r1, w0, w1 = (ref[i : i + 1, :] for i in range(4))
        m = jnp.where(r0 == who, 1.0, jnp.where(r1 == who, 1.0, 0.0))
        place = dot(m, upper, 1, 0)
        share = jnp.where(r0 == who, w0, jnp.where(r1 == who, w1, 0.0))
        for k in range(HALF):
            hit = jnp.where(slot == place[k : k + 1, :], m[k : k + 1, :], 0.0)
            oh[b, k * SLOT : (k + 1) * SLOT, :] = hit.astype(BF16)
            ws = jnp.sum(hit * share[k : k + 1, :], axis=1, keepdims=True)
            wcol[k, b * SLOT : (b + 1) * SLOT, :] = jnp.broadcast_to(ws, (SLOT, 256))
        oht[b] = oh[b].T

    serve("sent")

    def squares(src):
        v = land[src].astype(F32)
        v = v * v
        return v[:, 0:128] + v[:, 128:256] + v[:, 256:384] + v[:, 384:512]

    acc = squares(me_e)
    for dz, dx in FAR:
        src = peer(4 - dz, 4 - dx)
        rcopy(land.at[src], land.at[src], tk_s.at[src], tk_r.at[src], {"exp": src}).wait_recv()
        acc = acc + squares(src)
    serve("arrived")
    rs = lax.rsqrt(jnp.sum(acc, axis=1, keepdims=True) * (1.0 / 8192.0) + EPS)

    def near(src):
        return rcopy(tok.at[0, src], tok.at[1, src], nb_s.at[src], nb_r.at[src], {"seq": sib})

    def normal(src, _):
        tok[0, src] = (land[src].astype(F32) * rs).astype(BF16)
        near(src).start()
        return 0

    lax.fori_loop(0, 16, normal, 0, unroll=2)
    mixed_cp.wait()

    def gather(b):
        def one(src, _):
            x = dot(oh[b], tok[b, src], 1, 0).astype(BF16)
            for k in range(HALF):
                rows = pl.ds(pl.multiple_of(k * 1024 + src * 64 + b * SLOT, SLOT), SLOT)
                xall[rows, :] = x[k * SLOT : (k + 1) * SLOT]
            return 0

        return one

    lax.fori_loop(0, 16, gather(0), 0, unroll=4)
    serve("near")

    def settle(src, _):
        near(src).wait()
        return 0

    lax.fori_loop(0, 16, settle, 0)
    lax.fori_loop(0, 16, gather(1), 0, unroll=4)

    for dz, dx in FAR:
        token_copy(peer(dz, dx)).wait_send()

    def expert(step, _):
        far = step // 4
        near_row = weights.near_row.astype(jnp.int32)
        e = (near_row + far - 2 * near_row * far) * 4 + lax.rem(step + weights.x, 4)
        for when in range(8):
            if SERVE.get(when):
                @pl.when(step == when)
                def _(when=when):
                    serve(when)
        weights.wait_y(e)
        for g in range(8):
            base = e * 1024 + g * 128
            x0 = xall[pl.ds(pl.multiple_of(base, 64), 64), :]
            x1 = xall[pl.ds(pl.multiple_of(base + 64, 64), 64), :]
            x = jnp.concatenate([x0[:, 0:256], x0[:, 256:512], x1[:, 0:256], x1[:, 256:512]], axis=0)
            for m in range(2):
                mid = dot(wbuf[e, m * 256 : m * 256 + 256, :], x, 1, 1)
                for hf, u in enumerate(swap_blocks(mid.reshape(32, 8, 256))):
                    u = u.reshape(8, 2, 16, 128)
                    rows = pl.ds((2 * g + hf) * 16, 16)
                    rbuf[m, :, rows, 0:128] = u[:, 0]
                    rbuf[m, :, rows, 128:256] = u[:, 1]
        for g in range(8):
            for t in range(3):
                up = dot(wbuf[e, 512 + t * 256 : 768 + t * 256, :], rbuf[0, g], 1, 0)
                gt = dot(wbuf[e, 1280 + t * 256 : 1536 + t * 256, :], rbuf[1, g], 1, 0)
                hbuf[g, t * 256 : t * 256 + 256, :] = (silu(gt) * up).astype(BF16)
        for g in range(8):
            mid = sum(
                dot(wbuf[e, 2048 + t * 256 : 2304 + t * 256, :], hbuf[g, t * 256 : t * 256 + 256, :], 1, 0)
                for t in range(3)
            )
            for hf, u in enumerate(swap_blocks(mid.reshape(32, 8, 256))):
                u = u.reshape(8, 2, 16, 128)
                rows = pl.ds((2 * g + hf) * 16, 16)
                r2[:, rows, 0:128] = u[:, 0]
                r2[:, rows, 128:256] = u[:, 1]
        wc = wcol[e]
        wc = jnp.concatenate([wc, wc, wc, wc], axis=0)
        for g in range(8):
            o = (dot(r2[g], wbuf[e, 2816:3072, :], 0, 0) * wc).astype(BF16).reshape(4, 2, SLOT, 256)
            for q in range(4):
                for b in range(2):
                    rows = pl.ds(pl.multiple_of(e * SLOT + ((2 * g + q // 2) * 2 + b) * 256, SLOT), SLOT)
                    big[rows, (q % 2) * 256 : (q % 2) * 256 + 256] = o[q, b]
        return 0

    lax.fori_loop(0, HALF, expert, 0)

    def part(t, b):
        return dot(oht[b], big[pl.ds(pl.multiple_of((2 * t + b) * 256, 256), 256), :], 1, 0)

    def part_copy(t):
        return rcopy(other.at[t], theirs.at[t], pa_s.at[t], pa_r.at[t], {"seq": sib})

    def out_copy(t):
        cols = pl.ds(pl.multiple_of(t * 512, 512), 512)
        return pltpu.make_async_copy(result.at[t], routed_h.at[:, cols], ro_s.at[t])

    def give(t, _):
        other[t] = part(t, 1).astype(BF16)
        part_copy(t).start()
        return 0

    lax.fori_loop(0, 16, give, 0, unroll=4)

    def take(t, _):
        mine = part(t, 0)
        part_copy(t).wait()
        result[t] = (mine + theirs[t].astype(F32)).astype(BF16)
        out_copy(t).start()
        return 0

    lax.fori_loop(0, 16, take, 0, unroll=4)

    def done(t, _):
        out_copy(t).wait()
        return 0

    lax.fori_loop(0, 16, done, 0)
    for d in range(1, 8):
        @pl.when(me_s + d < 8)
        def _(d=d):
            state_copy(d, me_s + d).wait_send()
    for cp in sq_cp:
        cp.wait_send()
    weights.drain()


def run(*operands):
    vm = pl.BlockSpec(memory_space=pltpu.VMEM)
    hbm = pl.BlockSpec(memory_space=pl.ANY)
    dma = pltpu.SemaphoreType.DMA
    return pl.pallas_call(
        kernel,
        out_shape=(jax.ShapeDtypeStruct((2048, WID), BF16), jax.ShapeDtypeStruct((CH, 8192), BF16)),
        in_specs=[hbm, hbm, vm, vm, vm, vm, vm, vm, hbm, vm, vm] + [hbm] * 6,
        out_specs=(hbm, hbm),
        scratch_shapes=[
            pltpu.VMEM((2048, WID), F32),
            pltpu.VMEM((8192, WID), BF16),
            pltpu.VMEM((NCH, 16, WID), F32),
            pltpu.VMEM((CH, 2 * CH), BF16),
            pltpu.VMEM((CH, 2 * CH), BF16),
            pltpu.VMEM((NCH, WID), F32),
            pltpu.VMEM((NCH, WID), F32),
            pltpu.VMEM((NCH, WID), F32),
            pltpu.VMEM((32, WID), BF16),
            pltpu.VMEM((8, 32, WID), BF16),
            pltpu.VMEM((16, NCH, CH), F32),
            pltpu.VMEM((16, CH, WID), BF16),
            pltpu.VMEM((CH, 2 * CH), BF16),
            pltpu.VMEM((8, CH), F32),
            pltpu.VMEM((8, CH), F32),
            pltpu.VMEM((2, 256, 768), BF16),
            pltpu.VMEM((2, 256, 256), BF16),
            pltpu.VMEM((768, 256), BF16),
            pltpu.VMEM((2, 16, CH, WID), BF16),
            pltpu.VMEM((8192, WID), BF16),
            pltpu.VMEM((2, 256, CH), BF16),
            pltpu.VMEM((2, CH, 256), BF16),
            pltpu.VMEM((HALF, 64, 256), F32),
            pltpu.VMEM((2, 8, 256, 256), BF16),
            pltpu.VMEM((8, 256, 256), BF16),
            pltpu.VMEM((8, 768, 256), BF16),
            pltpu.VMEM((HALF, PACK, 256), BF16),
            pltpu.VMEM((16, CH, WID), BF16),
            pltpu.VMEM((16, CH, WID), BF16),
            pltpu.VMEM((16, CH, WID), BF16),
            dma((3,)), dma((8,)), dma((8,)), dma((16,)), dma((16,)), dma((16,)), dma((16,)), dma((16,)), dma((16,)),
            dma, dma,
            dma((128,)), dma((8, 2)), dma((8, 2)), dma((8, 4)), dma((6,)), dma, dma((16,)), dma((16,)), dma((16,)),
        ],
        compiler_params=pltpu.CompilerParams(
            collective_id=0, has_side_effects=True, vmem_limit_bytes=61 * 1024 * 1024
        ),
        name="mixer_experts",
    )(*operands)


def body(
    signal, out_gate, state_in, state_out, step_size, head_log_decay, skip_gain, norm_gain, residual,
    route, combine_weight, up_first, up_second, gate_first, gate_second, down_first, down_second,
):
    return run(
        signal, out_gate, state_in.T, state_out.T, step_size, head_log_decay, skip_gain.reshape(1, 8),
        norm_gain.reshape(1, WID), residual, route.T, combine_weight,
        up_first, up_second, gate_first, gate_second, down_first, down_second,
    )


def solution(mesh):
    in_specs = (
        P("seq", "exp"), P("seq", "exp"), P("seq", None), P("seq", None), P("exp", "seq"), P("exp", "seq"),
        P("exp"), P("exp"), P("seq", "exp"), P(("seq", "exp"), None), P(None, ("seq", "exp")),
        P("exp", None, None), P("exp", None, None), P("exp", None, None), P("exp", None, None),
        P("exp", None, None), P("exp", None, None),
    )
    out_specs = (P("seq", "exp"), P(("seq", "exp"), None))
    return jax.shard_map(body, mesh=mesh, in_specs=in_specs, out_specs=out_specs, check_vma=False)
```

```python
import jax
import jax.numpy as jnp
from jax import lax
from jax.experimental import pallas as pl
from jax.experimental.pallas import tpu as pltpu
from jax.sharding import PartitionSpec as P

MESH = pl.DeviceIdType.MESH
HIGH = lax.Precision.HIGHEST
EPS = 1e-05
F32, BF16 = jnp.float32, jnp.bfloat16
CH = 128
NCH = 16
WID = 512
SLOT = 32
HALF = 8
PACK = 3072


def iota(shape, dim):
    return lax.broadcasted_iota(jnp.int32, shape, dim)


def dot(a, b, ca, cb, precision=None):
    return lax.dot_general(
        a, b, (((ca,), (cb,)), ((), ())), precision=precision, preferred_element_type=F32
    )


def halves(v):
    hi = v.astype(BF16)
    return hi, (v - hi.astype(F32)).astype(BF16)


def rcopy(src, dst, send, recv, dev):
    return pltpu.make_async_remote_copy(
        src_ref=src, dst_ref=dst, send_sem=send, recv_sem=recv, device_id=dev, device_id_type=MESH
    )


def silu(v):
    return v * (0.5 + 0.5 * jnp.tanh(0.5 * v))


NF = 768
NY = PACK - 3 * NF
FAR = ((2, 2), (1, 2), (2, 1), (2, 3), (3, 2), (1, 1), (3, 3), (1, 3), (3, 1), (0, 2), (2, 0), (0, 1), (0, 3), (1, 0), (3, 0))
U1, U2 = 8, 8


def swap_blocks(v):
    n = v.shape[0]
    v = v.reshape(n // 2, 2, 8, 256)
    left = iota((n // 2, 8, 128), 2) < 64
    out = []
    for hf in range(2):
        v0 = v[:, 0, :, hf * 128 : hf * 128 + 128]
        v1 = v[:, 1, :, hf * 128 : hf * 128 + 128]
        u0 = jnp.where(left, v0, pltpu.roll(v1, 64, 2))
        u1 = jnp.where(left, pltpu.roll(v0, 64, 2), v1)
        out.append(jnp.concatenate([u0, u1], axis=1).astype(BF16))
    return out


class Weights:
    def __init__(self, me_e, me_s, wbuf, send, f_sem, b_sem, y_sem):
        self.core = lax.rem(me_s, 2)
        self.z, self.x = me_e // 4, lax.rem(me_e, 4)
        self.row = lax.rem(self.z + 4 - 2 * self.core, 4)
        self.odd = lax.rem(me_s // 2, 2)
        self.me_s = me_s
        self.wbuf, self.send = wbuf, send
        self.f_sem, self.b_sem, self.y_sem = f_sem, b_sem, y_sem
        self.own = lax.rem(self.row, 2) * 4 + self.x
        self.near_row = (self.row == 1) | (self.row == 2)
        self.is_src = self.row < 2
        self.sent = []
        self.known = {(dz, dx): self.valid(dz, dx) for dz in range(4) for dx in range(4)}

    def to(self, axis, step):
        if axis == "x":
            return {"exp": self.z * 4 + lax.rem(self.x + 4 + step, 4)}
        if axis == "z":
            return {"exp": lax.rem(self.z + 4 + step, 4) * 4 + self.x}
        return {"seq": lax.rem(self.me_s + 8 + 2 * step, 8)}

    def valid(self, dz, dx):
        r = lax.rem(self.row + 4 - dz, 4)
        return r < 2, lax.rem(r, 2) * 4 + lax.rem(self.x + 4 - dx, 4)

    def rows(self, tree, half):
        base = self.odd * (PACK - NF) if tree == "f" else NF + self.odd * (PACK - 3 * NF)
        n = NF if half is None else NF // 2
        return pl.ds(pl.multiple_of(base + (half or 0) * (NF // 2), 64), n)

    def y_rows(self, tree, half, odd):
        base, n = (odd * (PACK - NF), NF) if tree == "f" else (NF + odd * (PACK - 2 * NF - NY), NY)
        return pl.ds(pl.multiple_of(base + half * (n // 2), 64), n // 2)

    def push(self, ok, k, tree, half, axis, step):
        number = len(self.sent)

        def make():
            rows = self.y_rows(tree, half, self.odd) if axis == "y" else self.rows(tree, half)
            ref = self.wbuf.at[k, rows]
            sem = (self.f_sem if tree == "f" else self.b_sem).at[k, half or 0]
            if axis == "y":
                sem = self.y_sem.at[k, half + (0 if tree == "f" else 2)]
            return rcopy(ref, ref, self.send.at[number], sem, self.to(axis, step))

        make().start()
        self.sent.append((ok, make))

    def start(self):
        @pl.when(self.is_src)
        def _():
            for tree, axes in (("f", "xz"), ("b", "zx")):
                self.push(self.is_src, self.own, tree, None, axes[0], 1)
                self.push(self.is_src, self.own, tree, None, axes[0], -1)
            for tree, axis in (("f", "z"), ("b", "x")):
                self.push(self.is_src, self.own, tree, None, axis, 1)
                self.push(self.is_src, self.own, tree, None, axis, -1)

    def service(self, tree, first, second):
        dz, dx = (second, first) if tree == "f" else (first, second)
        ax1, ax2 = ("x", "z") if tree == "f" else ("z", "x")
        ok, k = self.known[dz, dx]
        sem = self.f_sem if tree == "f" else self.b_sem

        @pl.when(ok)
        def _():
            two = second == 2 or (second == 0 and first == 2)
            for half in (0, 1) if two else (None,):
                ref = self.wbuf.at[k, self.rows(tree, half)]
                rcopy(ref, ref, self.send.at[0], sem.at[k, half or 0], self.to("x", 1)).wait_recv()
            if second == 0:
                if first == 1:
                    self.push(ok, k, tree, 0, ax1, 1)
                if first == 3:
                    self.push(ok, k, tree, 1, ax1, -1)
                self.push(ok, k, tree, None, ax2, 1)
                self.push(ok, k, tree, None, ax2, -1)
            if second == 1:
                self.push(ok, k, tree, 0, ax2, 1)
            if second == 3:
                self.push(ok, k, tree, 1, ax2, -1)
            if tree == "f" or NY:
                self.push(ok, k, tree, 0, "y", 1)
                self.push(ok, k, tree, 1, "y", -1)

    def wait_y(self, k):
        @pl.when(jnp.logical_or(k != self.own, jnp.logical_not(self.is_src)))
        def _():
            for part in range(4 if NY else 2):
                ref = self.wbuf.at[k, self.y_rows("fb"[part // 2], part % 2, 1 - self.odd)]
                rcopy(ref, ref, self.send.at[0], self.y_sem.at[k, part], self.to("y", 1)).wait_recv()

    def drain(self):
        for ok, make in self.sent:
            @pl.when(ok)
            def _(make=make):
                make().wait_send()


SERVE = {
    "state": (("f", 1, 0), ("b", 1, 0), ("f", 3, 0), ("b", 3, 0)),
    "ssq": (("f", 2, 0), ("b", 0, 1), ("b", 0, 3), ("f", 0, 1), ("f", 0, 3), ("b", 2, 0)),
    "sent": (("f", 1, 1), ("f", 1, 3), ("f", 3, 1), ("f", 3, 3), ("b", 1, 1), ("b", 1, 3), ("b", 3, 1), ("b", 3, 3)),
    "arrived": (("f", 2, 1), ("f", 2, 3), ("b", 0, 2), ("b", 1, 2), ("b", 3, 2)),
    "near": (("b", 2, 1), ("b", 2, 3), ("f", 0, 2)),
    2: (("f", 1, 2), ("f", 3, 2), ("f", 2, 2), ("b", 2, 2)),
}


def kernel(
    sig_h, gate_h, b_in, c_out, dt, rate, skip, ngain, resid_h, route, share_in,
    uf_h, us_h, gf_h, gs_h, df_h, ds_h,
    mixed_h, routed_h,
    sig, big, sraw, amat, bmat, gtot, gend, gmid, st_loc, st_buf, ssq, land, inv_s, info, info_l, raw_f, raw_s, raw_d,
    land2, xall, oh, oht, wcol, rcol, scale, rbuf, r2, hbuf, wbuf, other, theirs, result,
    ld_s, st_s, st_r, sq_s, sq_r, tk_s, tk_r, nb_s, nb_r, in_s, in_r, sc_s, sc_r,
    w_s, f_r, b_r, y_r, rw_s, mx_s, pa_s, pa_r, ro_s,
):
    me_e, me_s = lax.axis_index("exp"), lax.axis_index("seq")
    core = lax.rem(me_s, 2)
    sib = me_s + 1 - 2 * core
    gate, resid, bx, sendb = (big.at[i * 2048 : (i + 1) * 2048] for i in range(4))
    loads = [
        pltpu.make_async_copy(sig_h, sig, ld_s.at[0]),
        pltpu.make_async_copy(gate_h, gate, ld_s.at[1]),
        pltpu.make_async_copy(resid_h, resid, ld_s.at[2]),
    ]
    weights = Weights(me_e, me_s, wbuf, w_s, f_r, b_r, y_r)
    mine = wbuf.at[weights.own]
    raws = [
        pltpu.make_async_copy(us_h.at[0], raw_s.at[0], rw_s.at[0]),
        pltpu.make_async_copy(gs_h.at[0], raw_s.at[1], rw_s.at[1]),
        pltpu.make_async_copy(uf_h.at[0], raw_f.at[0], rw_s.at[2]),
        pltpu.make_async_copy(gf_h.at[0], raw_f.at[1], rw_s.at[3]),
        pltpu.make_async_copy(ds_h.at[0], raw_d, rw_s.at[4]),
        pltpu.make_async_copy(df_h.at[0], mine.at[2816:3072], rw_s.at[5]),
    ]

    @pl.when(weights.is_src)
    def _():
        for cp in raws:
            cp.start()

    for cp in loads:
        cp.start()

    barrier = pltpu.get_barrier_semaphore()
    for d in range(1, 16):
        pl.semaphore_signal(barrier, inc=1, device_id={"exp": lax.rem(me_e + d, 16)}, device_id_type=MESH)
    for d in range(1, 8):
        pl.semaphore_signal(barrier, inc=1, device_id={"seq": lax.rem(me_s + d, 8)}, device_id_type=MESH)
    info[...] = jnp.concatenate([route[...].astype(F32), share_in[...], jnp.zeros((4, CH), F32)], axis=0)

    @pl.when(weights.is_src)
    def _():
        for cp in raws:
            cp.wait()
        for i in range(2):
            mine[i * 256 : i * 256 + 256, :] = raw_s[i].T
            for t in range(3):
                mine[512 + (3 * i + t) * 256 : 768 + (3 * i + t) * 256, :] = raw_f[i, :, t * 256 : t * 256 + 256].T
        for t in range(3):
            mine[2048 + t * 256 : 2304 + t * 256, :] = raw_d[t * 256 : t * 256 + 256, :].T


    def serve(when):
        for unit in SERVE.get(when, ()):
            weights.service(*unit)

    rate2 = jnp.concatenate([rate[:, c * CH : (c + 1) * CH] for c in range(NCH)], axis=0)
    dt2 = jnp.concatenate([dt[:, c * CH : (c + 1) * CH] for c in range(NCH)], axis=0)
    tri = (iota((CH, CH), 0) >= iota((CH, CH), 1)).astype(F32)
    run = dot(tri, rate2, 1, 1, HIGH)
    mid, end = run[63:64, :], run[127:128, :]
    av = jnp.exp(mid - run)
    bv = jnp.exp(run - mid) * dt2.T
    ah, al = halves(av)
    bh, bl = halves(bv)
    amat[:, :CH], amat[:, CH:] = ah, al
    bmat[:, :CH], bmat[:, CH:] = bh, bl
    spread = ((iota((CH, WID), 0) & 7) == (iota((CH, WID), 1) >> 6)).astype(F32)
    own = (iota((NCH, CH), 1) >> 3) == iota((NCH, CH), 0)

    def rows_of(v):
        return dot(jnp.where(own, v, 0.0), spread, 1, 0, HIGH)

    gtot[...] = rows_of(jnp.exp(-end))
    gend[...] = rows_of(jnp.exp(mid - end))
    gmid[...] = rows_of(jnp.exp(-mid))
    all_end = dot(jnp.broadcast_to(end, (8, CH)), spread, 1, 0, HIGH)

    pl.semaphore_wait(barrier, 22)
    info_cp = rcopy(info, info_l, in_s, in_r, {"seq": sib})
    info_cp.start()
    weights.start()

    def picker(c):
        return ((iota((2 * CH, WID), 0) & (CH - 1)) == c * 8 + (iota((2 * CH, WID), 1) >> 6)).astype(BF16)

    loads[0].wait()

    def first(c, state):
        rows = pl.ds(pl.multiple_of(c * CH, CH), CH)
        x = (dot(bmat[...], picker(c), 1, 0) * sig[rows, :]).astype(BF16)
        bx[rows, :] = x
        s = dot(b_in[:, rows].astype(BF16), x, 1, 0)
        sraw[c] = s
        return gtot[pl.ds(c, 1), :] * state + gend[pl.ds(c, 1), :] * s

    state = lax.fori_loop(0, NCH, first, jnp.zeros((16, WID), F32), unroll=U1)
    gh, gl = halves(jnp.exp(-all_end))
    st_loc[...] = jnp.concatenate([state.astype(BF16), gh, gl], axis=0)
    st_buf[me_s] = st_loc[...]

    def state_copy(d, to):
        return rcopy(st_loc, st_buf.at[me_s], st_s.at[d], st_r.at[me_s], {"seq": to})

    for d in range(1, 8):
        @pl.when(me_s + d < 8)
        def _(d=d):
            state_copy(d, me_s + d).start()
    loads[1].wait()
    loads[2].wait()
    serve("state")
    for d in range(1, 8):
        @pl.when(me_s >= d)
        def _(d=d):
            frm = me_s - d
            rcopy(st_loc, st_buf.at[frm], st_s.at[d], st_r.at[frm], {"seq": frm}).wait_recv()

    state = jnp.zeros((16, WID), F32)
    for k in range(7):
        got = st_buf[k].astype(F32)
        state = jnp.where(k < me_s, (got[16:17] + got[24:25]) * state + got[0:16], state)

    low = iota((CH, CH), 0) >= iota((CH, CH), 1)
    skip_e = dot(jnp.broadcast_to(skip[...], (8, 8)), spread[0:8, :], 1, 0, HIGH)[0:1, :]
    ones = jnp.ones((8, WID), BF16)

    def second(c, state):
        rows = pl.ds(pl.multiple_of(c * CH, CH), CH)
        cm = c_out[:, rows].astype(BF16)
        scores = jnp.where(low, dot(cm, b_in[:, rows].astype(BF16), 0, 0), 0.0).astype(BF16)
        enter = (gmid[pl.ds(c, 1), :] * state).astype(BF16)
        y = dot(scores, bx[rows, :], 1, 0) + dot(cm, enter, 0, 0)
        y = y * dot(amat[...], picker(c), 1, 0) + skip_e * sig[rows, :]
        g = y * silu(gate[rows, :].astype(F32))
        sig[rows, :] = g
        ssq[me_e, pl.ds(c, 1), :] = dot(ones, (g * g).astype(BF16), 1, 1)[0:1, :]
        return gtot[pl.ds(c, 1), :] * state + gend[pl.ds(c, 1), :] * sraw[c]

    lax.fori_loop(0, NCH, second, state, unroll=U2)

    sq_cp = []
    for d in range(1, 16):
        to = lax.rem(me_e + d, 16)
        sq_cp.append(rcopy(ssq.at[me_e], ssq.at[me_e], sq_s.at[d], sq_r.at[me_e], {"exp": to}))
        sq_cp[-1].start()
    serve("ssq")
    for d in range(1, 16):
        frm = lax.rem(me_e + 16 - d, 16)
        rcopy(ssq.at[frm], ssq.at[frm], sq_s.at[d], sq_r.at[frm], {"exp": frm}).wait_recv()
    total = ssq[0]
    for k in range(1, 16):
        total = total + ssq[k]
    inv = lax.rsqrt(total * (1.0 / 8192.0) + EPS)
    inv_t = jnp.concatenate([inv, jnp.zeros((CH - NCH, CH), F32)], axis=0).T
    ih, il = halves(inv_t)
    inv_s[:, :CH], inv_s[:, CH:] = ih, il

    def third(c):
        rows = pl.ds(pl.multiple_of(c * CH, CH), CH)
        sel = ((iota((2 * CH, WID), 0) & (CH - 1)) == c).astype(BF16)
        m = (sig[rows, :] * dot(inv_s[...], sel, 1, 0) * ngain[...]).astype(BF16)
        xall[rows, :] = m
        return (resid[rows, :].astype(F32) + m.astype(F32)).astype(BF16)

    def token_copy(c):
        rows = pl.ds(pl.multiple_of(c * CH, CH), CH)
        return rcopy(sendb.at[rows], land.at[me_e], tk_s.at[c], tk_r.at[me_e], {"exp": c})

    def peer(dz, dx):
        return lax.rem(weights.z + dz, 4) * 4 + lax.rem(weights.x + dx, 4)

    for dz, dx in FAR:
        c = peer(dz, dx)
        sendb[pl.ds(pl.multiple_of(c * CH, CH), CH), :] = third(c)
        token_copy(c).start()
    land[me_e] = third(me_e)
    mixed_cp = pltpu.make_async_copy(xall.at[0:2048], mixed_h, mx_s)
    mixed_cp.start()

    info_cp.wait()
    shift = (core * HALF).astype(F32)
    upper = (iota((CH, CH), 0) < iota((CH, CH), 1)).astype(F32)
    who = iota((HALF, CH), 0).astype(F32) + shift
    slot = iota((SLOT, CH), 0).astype(F32)
    for b, ref in enumerate((info, info_l)):
        r0, r1, w0, w1 = (ref[i : i + 1, :] for i in range(4))
        m = jnp.where(r0 == who, 1.0, jnp.where(r1 == who, 1.0, 0.0))
        place = dot(m, upper, 1, 0)
        share = jnp.where(r0 == who, w0, jnp.where(r1 == who, w1, 0.0))
        for k in range(HALF):
            hit = jnp.where(slot == place[k : k + 1, :], m[k : k + 1, :], 0.0)
            oh[b, k * SLOT : (k + 1) * SLOT, :] = hit.astype(BF16)
            ws = jnp.sum(hit * share[k : k + 1, :], axis=1, keepdims=True)
            wcol[k, b * SLOT : (b + 1) * SLOT, :] = jnp.broadcast_to(ws, (SLOT, 256))
        oht[b] = oh[b].T

    serve("sent")

    def squares(src):
        v = land[src].astype(F32)
        v = v * v
        return v[:, 0:128] + v[:, 128:256] + v[:, 256:384] + v[:, 384:512]

    def near(src):
        return rcopy(land.at[src], land2.at[src], nb_s.at[src], nb_r.at[src], {"seq": sib})

    def gather(b, src):
        x = dot(oh[b], (land2 if b else land)[src], 1, 0).astype(BF16)
        for k in range(HALF):
            rows = pl.ds(pl.multiple_of(k * 1024 + src * 64 + b * SLOT, SLOT), SLOT)
            xall[rows, :] = x[k * SLOT : (k + 1) * SLOT]

    near(me_e).start()
    mixed_cp.wait()
    acc = squares(me_e)
    gather(0, me_e)
    for dz, dx in FAR:
        src = peer(4 - dz, 4 - dx)
        rcopy(land.at[src], land.at[src], tk_s.at[src], tk_r.at[src], {"exp": src}).wait_recv()
        near(src).start()
        acc = acc + squares(src)
        gather(0, src)
    total = dot(jnp.ones((8, CH), F32), acc, 1, 1, HIGH)
    scale[0] = lax.rsqrt(total * (1.0 / 8192.0) + EPS)
    scale_cp = rcopy(scale.at[0], scale.at[1], sc_s, sc_r, {"seq": sib})
    scale_cp.start()
    serve("arrived")
    near(me_e).wait()
    gather(1, me_e)
    for dz, dx in FAR:
        src = peer(4 - dz, 4 - dx)
        near(src).wait()
        gather(1, src)
    scale_cp.wait()
    for b in range(2):
        for k in range(HALF):
            hit = oh[b, k * SLOT : (k + 1) * SLOT, :].astype(F32)
            rs = jnp.sum(hit * scale[b, 0:1, :], axis=1, keepdims=True)
            rcol[k, b * SLOT : (b + 1) * SLOT, :] = jnp.broadcast_to(rs, (SLOT, 256))
    serve("near")

    for dz, dx in FAR:
        token_copy(peer(dz, dx)).wait_send()

    def expert(step, _):
        far, turn = step // 4, lax.rem(step, 4)
        turn = jnp.where(turn == 2, 3, jnp.where(turn == 3, 2, turn))
        near_row = weights.near_row.astype(jnp.int32)
        e = (near_row + far - 2 * near_row * far) * 4 + lax.rem(turn + weights.x, 4)
        for when in range(8):
            if SERVE.get(when):
                @pl.when(step == when)
                def _(when=when):
                    serve(when)
        weights.wait_y(e)
        rc = rcol[e]
        for g in range(8):
            base = e * 1024 + g * 128
            x0 = xall[pl.ds(pl.multiple_of(base, 64), 64), :]
            x1 = xall[pl.ds(pl.multiple_of(base + 64, 64), 64), :]
            x = jnp.concatenate(
                [(v.astype(F32) * rc).astype(BF16) for v in (x0[:, 0:256], x0[:, 256:512], x1[:, 0:256], x1[:, 256:512])],
                axis=0,
            )
            for m in range(2):
                mid = dot(wbuf[e, m * 256 : m * 256 + 256, :], x, 1, 1)
                for hf, u in enumerate(swap_blocks(mid.reshape(32, 8, 256))):
                    u = u.reshape(8, 2, 16, 128)
                    rows = pl.ds((2 * g + hf) * 16, 16)
                    rbuf[m, :, rows, 0:128] = u[:, 0]
                    rbuf[m, :, rows, 128:256] = u[:, 1]
        for g in range(8):
            for t in range(3):
                up = dot(wbuf[e, 512 + t * 256 : 768 + t * 256, :], rbuf[0, g], 1, 0)
                gt = dot(wbuf[e, 1280 + t * 256 : 1536 + t * 256, :], rbuf[1, g], 1, 0)
                hbuf[g, t * 256 : t * 256 + 256, :] = (silu(gt) * up).astype(BF16)
        for g in range(8):
            mid = sum(
                dot(wbuf[e, 2048 + t * 256 : 2304 + t * 256, :], hbuf[g, t * 256 : t * 256 + 256, :], 1, 0)
                for t in range(3)
            )
            for hf, u in enumerate(swap_blocks(mid.reshape(32, 8, 256))):
                u = u.reshape(8, 2, 16, 128)
                rows = pl.ds((2 * g + hf) * 16, 16)
                r2[:, rows, 0:128] = u[:, 0]
                r2[:, rows, 128:256] = u[:, 1]
        wc = wcol[e]
        wc = jnp.concatenate([wc, wc, wc, wc], axis=0)
        for g in range(8):
            o = (dot(r2[g], wbuf[e, 2816:3072, :], 0, 0) * wc).astype(BF16).reshape(4, 2, SLOT, 256)
            for q in range(4):
                for b in range(2):
                    rows = pl.ds(pl.multiple_of(e * SLOT + ((2 * g + q // 2) * 2 + b) * 256, SLOT), SLOT)
                    big[rows, (q % 2) * 256 : (q % 2) * 256 + 256] = o[q, b]
        return 0

    lax.fori_loop(0, HALF, expert, 0)

    def part(t, b):
        return dot(oht[b], big[pl.ds(pl.multiple_of((2 * t + b) * 256, 256), 256), :], 1, 0)

    def part_copy(t):
        return rcopy(other.at[t], theirs.at[t], pa_s.at[t], pa_r.at[t], {"seq": sib})

    def out_copy(t):
        cols = pl.ds(pl.multiple_of(t * 512, 512), 512)
        return pltpu.make_async_copy(result.at[t], routed_h.at[:, cols], ro_s.at[t])

    def give(t, _):
        other[t] = part(t, 1).astype(BF16)
        part_copy(t).start()
        return 0

    lax.fori_loop(0, 16, give, 0, unroll=4)

    def take(t, _):
        mine = part(t, 0)
        part_copy(t).wait()
        result[t] = (mine + theirs[t].astype(F32)).astype(BF16)
        out_copy(t).start()
        return 0

    lax.fori_loop(0, 16, take, 0, unroll=4)

    def done(t, _):
        out_copy(t).wait()
        return 0

    lax.fori_loop(0, 16, done, 0)
    for d in range(1, 8):
        @pl.when(me_s + d < 8)
        def _(d=d):
            state_copy(d, me_s + d).wait_send()
    for cp in sq_cp:
        cp.wait_send()
    weights.drain()


def run(*operands):
    vm = pl.BlockSpec(memory_space=pltpu.VMEM)
    hbm = pl.BlockSpec(memory_space=pl.ANY)
    dma = pltpu.SemaphoreType.DMA
    return pl.pallas_call(
        kernel,
        out_shape=(jax.ShapeDtypeStruct((2048, WID), BF16), jax.ShapeDtypeStruct((CH, 8192), BF16)),
        in_specs=[hbm, hbm, vm, vm, vm, vm, vm, vm, hbm, vm, vm] + [hbm] * 6,
        out_specs=(hbm, hbm),
        scratch_shapes=[
            pltpu.VMEM((2048, WID), F32),
            pltpu.VMEM((8192, WID), BF16),
            pltpu.VMEM((NCH, 16, WID), F32),
            pltpu.VMEM((CH, 2 * CH), BF16),
            pltpu.VMEM((CH, 2 * CH), BF16),
            pltpu.VMEM((NCH, WID), F32),
            pltpu.VMEM((NCH, WID), F32),
            pltpu.VMEM((NCH, WID), F32),
            pltpu.VMEM((32, WID), BF16),
            pltpu.VMEM((8, 32, WID), BF16),
            pltpu.VMEM((16, NCH, CH), F32),
            pltpu.VMEM((16, CH, WID), BF16),
            pltpu.VMEM((CH, 2 * CH), BF16),
            pltpu.VMEM((8, CH), F32),
            pltpu.VMEM((8, CH), F32),
            pltpu.VMEM((2, 256, 768), BF16),
            pltpu.VMEM((2, 256, 256), BF16),
            pltpu.VMEM((768, 256), BF16),
            pltpu.VMEM((16, CH, WID), BF16),
            pltpu.VMEM((8192, WID), BF16),
            pltpu.VMEM((2, 256, CH), BF16),
            pltpu.VMEM((2, CH, 256), BF16),
            pltpu.VMEM((HALF, 64, 256), F32),
            pltpu.VMEM((HALF, 64, 256), F32),
            pltpu.VMEM((2, 8, CH), F32),
            pltpu.VMEM((2, 8, 256, 256), BF16),
            pltpu.VMEM((8, 256, 256), BF16),
            pltpu.VMEM((8, 768, 256), BF16),
            pltpu.VMEM((HALF, PACK, 256), BF16),
            pltpu.VMEM((16, CH, WID), BF16),
            pltpu.VMEM((16, CH, WID), BF16),
            pltpu.VMEM((16, CH, WID), BF16),
            dma((3,)), dma((8,)), dma((8,)), dma((16,)), dma((16,)), dma((16,)), dma((16,)), dma((16,)), dma((16,)),
            dma, dma, dma, dma,
            dma((128,)), dma((8, 2)), dma((8, 2)), dma((8, 4)), dma((6,)), dma, dma((16,)), dma((16,)), dma((16,)),
        ],
        compiler_params=pltpu.CompilerParams(
            collective_id=0, has_side_effects=True, vmem_limit_bytes=61 * 1024 * 1024
        ),
        name="mixer_experts",
    )(*operands)


def body(
    signal, out_gate, state_in, state_out, step_size, head_log_decay, skip_gain, norm_gain, residual,
    route, combine_weight, up_first, up_second, gate_first, gate_second, down_first, down_second,
):
    return run(
        signal, out_gate, state_in.T, state_out.T, step_size, head_log_decay, skip_gain.reshape(1, 8),
        norm_gain.reshape(1, WID), residual, route.T, combine_weight,
        up_first, up_second, gate_first, gate_second, down_first, down_second,
    )


def solution(mesh):
    in_specs = (
        P("seq", "exp"), P("seq", "exp"), P("seq", None), P("seq", None), P("exp", "seq"), P("exp", "seq"),
        P("exp"), P("exp"), P("seq", "exp"), P(("seq", "exp"), None), P(None, ("seq", "exp")),
        P("exp", None, None), P("exp", None, None), P("exp", None, None), P("exp", None, None),
        P("exp", None, None), P("exp", None, None),
    )
    out_specs = (P("seq", "exp"), P(("seq", "exp"), None))
    return jax.shard_map(body, mesh=mesh, in_specs=in_specs, out_specs=out_specs, check_vma=False)
```
